128 devices in a mesh: dp: 32 (over z, x, core), ep: 4 (over y).
Axes of the slice: x: 4, y: 4, z: 4, core: 2. Of those that a mesh axis runs over, the one named last changes fastest.
Arguments:
- query_rows: bfloat16 [128, 128, 576], P(('dp', 'ep')), may hold values from -65 to 65, as said below
- cache_latent: bfloat16 [524288, 576], P(('dp', 'ep')), may hold values from -6 to 6, as said below
- lengths: int32 [128], replicated, may hold values from 2 to 4096, as said below
- moe_input: bfloat16 [1024, 7168], P(('dp', 'ep')), may hold values from -6 to 6
- expert_ids: int32 [1024, 8], P(('dp', 'ep')), may hold values from 0 to 31, all different within a row; in each aligned block of 8 rows (0 to 7, 8 to 15, ...) at most 4 rows name the same one
- gate_weights: float32 [1024, 8], P(('dp', 'ep')), may hold values from 0.05 to 0.5
- expert_gate: bfloat16 [32, 7168, 1024], P('dp', None, 'ep'), may hold values from -0.0625 to 0.0625
- expert_up: bfloat16 [32, 7168, 1024], P('dp', None, 'ep'), may hold values from -0.0625 to 0.0625
- expert_down: bfloat16 [32, 1024, 7168], P('dp', 'ep'), may hold values from -0.1875 to 0.1875
Outputs:
- attn_out: bfloat16 [128, 128, 512], P(('dp', 'ep'))
- moe_out: bfloat16 [1024, 7168], P(('dp', 'ep'))
The draws below stay inside these ranges and needn't reach their ends.
Inputs may be any that keep to these rules, and one draw needn't show every extreme that they name: `lengths`: some request has exactly 4096 cached tokens in every draw. `expert_ids`: each row names 8 different experts. Among the rows of one device no expert is named more than 4 times, a bound that some block reaches. `cache_latent`: finite latent entries. `query_rows`: finite query entries.
All inputs are finite; a program needn't handle non-finite values.
Results may differ from the reference program's by a relative error of at most 0.008.
Values may be sent and summed in bfloat16 or wider, within the bound.
No kernel may reach another device: no remote copies, remote signals or barrier semaphores. Data moves between devices by JAX's collectives and lax.ppermute only.
A program may use at most 128 MiB of HBM per device.

```python
import math
import jax
import jax.numpy as jnp
import numpy as np
from jax import lax

WIDTH = 7168
HEADS = 128
LATENT = 512
KEY_DIM = 576
EXPERT_HIDDEN = 1024
TOPK = 8
EXPERTS = 32
MOE_TOK = 8
CAPACITY = 4
CTX_TOK = 4096
REQUESTS = 128
MOE_TOKENS = 1024
N_EP = 4


def joint_plan(key):
    base_key = jax.random.fold_in(key, 4242)
    keys_all = jax.random.split(base_key, 3)
    first = jax.random.randint(keys_all[0], (REQUESTS,), 0, CTX_TOK)
    second = jax.random.randint(keys_all[1], (REQUESTS,), 0, CTX_TOK)
    raw_lengths = first * second // CTX_TOK + 2
    chosen = jax.random.randint(keys_all[2], (), 0, REQUESTS)
    lengths = jnp.where(jnp.arange(REQUESTS, dtype=jnp.int32) == chosen, CTX_TOK, raw_lengths).astype(jnp.int32)
    return lengths


def draw_lengths(key, part):
    return joint_plan(key)


def draw_cache_latent(key, part):
    noise_key = jax.random.fold_in(key, 77)
    values = jnp.clip(jax.random.normal(noise_key, (REQUESTS, CTX_TOK, KEY_DIM), jnp.float32), -6.0, 6.0)
    return values.reshape(REQUESTS * CTX_TOK, KEY_DIM).astype(jnp.bfloat16)


def draw_query_rows(key, part):
    noise_key = jax.random.fold_in(key, 91)
    values = jnp.clip(jax.random.normal(noise_key, (REQUESTS, HEADS, KEY_DIM), jnp.float32), -6.0, 6.0)
    return values.astype(jnp.bfloat16)


def block_levels(own_key, dims, cuts, low, top_value):
    factor_of, own = 1.0, jax.random.fold_in(own_key, 6)
    for dim, blocks in cuts:
        heights = jnp.exp(jax.random.uniform(jax.random.fold_in(own, dim), (blocks,), jnp.float32, low / len(cuts), top_value / len(cuts)))
        factor_of = factor_of * jnp.repeat(heights, dims[dim] // blocks).reshape([-1 if axis == dim else 1 for axis in range(len(dims))])
    return factor_of


def deal_out(key, own, number, rows, number_of, top, limit, slope):
    sequence = jax.random.permutation(key, number_of)
    packed, usual = shares(number_of, rows * top, limit, slope, True), shares(number_of, rows * top, limit, slope, False)
    places = jnp.arange(number_of)

    def named(sizes, offset_by):
        used = int((sizes > 0).sum())
        fixed = max(1, used // 4)
        passed = fixed + (places - fixed + offset_by * (used - fixed)) % max(1, number_of - fixed)
        return jnp.zeros((number_of,), jnp.int32).at[sequence[jnp.where(places < fixed, places, passed)]].set(jnp.asarray(sizes, jnp.int32))

    sizes = jnp.where(number % 4 == 0, named(packed, number // 4), named(usual, number - number // 4 - 1))
    mixed = jax.random.permutation(jax.random.fold_in(own, 3), number_of)
    source_of, sink = mixed[0:number_of // 2 * 2:2], mixed[1:number_of // 2 * 2:2]
    room = jnp.minimum(sizes[source_of] - 1, limit - sizes[sink]) // 2
    room = jnp.where((source_of == sequence[0]) | (sink == sequence[0]) | (sizes[sink] == 0), 0, jnp.maximum(room, 0))
    passed = jax.random.randint(jax.random.fold_in(own, 4), (number_of // 2,), 0, 1 << 20) % (room + 1)
    sizes = sizes.at[source_of].add(-passed).at[sink].add(passed)
    labels = jnp.searchsorted(jnp.cumsum(sizes), jnp.arange(rows * top), side="right").astype(jnp.int32)
    listing = labels.reshape(top, rows).T
    listing = listing[jax.random.permutation(jax.random.fold_in(own, 1), rows)]
    offset_by = jax.random.randint(jax.random.fold_in(own, 2), (rows, 1), 0, top)
    return jnp.take_along_axis(listing, (jnp.arange(top)[None, :] + offset_by) % top, axis=1)


def shares(number_of, total, limit, skew, full):
    portions = [(1 << 20) // math.isqrt(standing ** skew) + 1 for standing in range(1, number_of + 1)]
    largest = limit if full else min(limit, max(-(-total // number_of), total * portions[0] // sum(portions)))
    least = 1 if total - largest >= number_of - 1 else 0
    holding, rest = [largest] + [least] * (number_of - 1), total - largest - least * (number_of - 1)
    while rest > 0:
        candidates = [i for i in range(1, number_of) if holding[i] < largest] or [i for i in range(1, number_of) if holding[i] < limit]
        pool, budget = sum([portions[i] for i in candidates]), rest
        for i in candidates:
            addition = min(limit - holding[i], max(1, budget * portions[i] // pool), rest)
            holding[i] = holding[i] + addition
            rest = rest - addition
    return np.array(holding)


def bell_draw(key, extent, spread, limit, shards=(), kind=jnp.bfloat16):
    array = spread * jax.random.normal(key, extent, jnp.float32)
    if shards:
        array = array * block_levels(key, extent, shards, -0.22, 0.18)
    return jnp.clip(array, -limit, limit).astype(kind)


def setup_inputs(seed: int = 0) -> dict:
    key_of = jax.random.split(jax.random.key(seed), 10)
    query_rows = draw_query_rows(jax.random.fold_in(key_of[9], 71), 0)
    cache_latent = draw_cache_latent(jax.random.fold_in(key_of[9], 71), 0)
    lengths = draw_lengths(jax.random.fold_in(key_of[9], 71), 0)
    moe_input = bell_draw(key_of[3], (MOE_TOKENS, WIDTH), 1.0, 6.0, ((0, 128),))
    expert_ids_keys = jax.random.split(jax.random.fold_in(key_of[4], 1), MOE_TOKENS // MOE_TOK)
    expert_ids_turns = jax.random.permutation(jax.random.fold_in(key_of[4], 3), MOE_TOKENS // MOE_TOK)
    expert_ids = jax.vmap(lambda own, number: deal_out(jax.random.fold_in(key_of[4], 2), own, number, MOE_TOK, EXPERTS, TOPK, CAPACITY, 2))(expert_ids_keys, expert_ids_turns).reshape((MOE_TOKENS, TOPK))
    gate_weights = jnp.clip(jnp.exp(math.log(0.5) - 2.3025851 * jax.random.uniform(key_of[5], (MOE_TOKENS, TOPK), jnp.float32) ** block_levels(key_of[5], (MOE_TOKENS, TOPK), ((0, 128),), -0.2, 0.2)), 0.05, 0.5)
    expert_gate = bell_draw(key_of[6], (EXPERTS, WIDTH, EXPERT_HIDDEN), WIDTH ** -0.5, 0.0625, ((0, 32), (2, 4)))
    expert_up = bell_draw(key_of[7], (EXPERTS, WIDTH, EXPERT_HIDDEN), WIDTH ** -0.5, 0.0625, ((0, 32), (2, 4)))
    expert_down = bell_draw(key_of[8], (EXPERTS, EXPERT_HIDDEN, WIDTH), EXPERT_HIDDEN ** -0.5, 0.1875, ((0, 32), (1, 4)))
    return {"query_rows": query_rows, "cache_latent": cache_latent, "lengths": lengths, "moe_input": moe_input, "expert_ids": expert_ids, "gate_weights": gate_weights, "expert_gate": expert_gate, "expert_up": expert_up, "expert_down": expert_down}


qk_scale = 192.0 ** -0.5


def attend_one(inputs):
    query_row, cache_rows, seq_length = inputs
    scores = qk_scale * jnp.dot(query_row, cache_rows.T, preferred_element_type=jnp.float32)
    live_mask = jnp.arange(CTX_TOK, dtype=jnp.int32)[None, :] < seq_length
    scores = jnp.where(live_mask, scores, -1e30)
    score_top = jnp.max(scores, axis=1, keepdims=True)
    exponent = jnp.where(live_mask, jnp.exp(scores - score_top), 0.0)
    weight_sum = jnp.sum(exponent, axis=1, keepdims=True)
    mixed_values = jnp.dot(exponent.astype(jnp.bfloat16), cache_rows[:, :LATENT], preferred_element_type=jnp.float32)
    return (mixed_values / weight_sum).astype(jnp.bfloat16)


def expert_rows(row_block, gate_proj, up_proj, down_proj):
    gate_act = jnp.dot(row_block, gate_proj, preferred_element_type=jnp.float32)
    up_act = jnp.dot(row_block, up_proj, preferred_element_type=jnp.float32)
    hidden = (jax.nn.silu(gate_act) * up_act).astype(jnp.bfloat16)
    group_size = EXPERT_HIDDEN // N_EP
    running_sum = jnp.zeros((row_block.shape[0], WIDTH), jnp.float32)
    for group_number in range(N_EP):
        lower = group_number * group_size
        partial_sum = jnp.dot(hidden[:, lower:lower + group_size], down_proj[lower:lower + group_size], preferred_element_type=jnp.float32)
        rounded = lax.optimization_barrier(partial_sum.astype(jnp.bfloat16))
        running_sum = running_sum + rounded.astype(jnp.float32)
    return running_sum.astype(jnp.bfloat16)


def reference(query_rows, cache_latent, lengths, moe_input, expert_ids, gate_weights, expert_gate, expert_up, expert_down):
    attn_out = lax.map(attend_one, (query_rows, cache_latent.reshape(REQUESTS, CTX_TOK, KEY_DIM), lengths))
    source_count = MOE_TOKENS // MOE_TOK
    slot_count = MOE_TOK * TOPK
    flat_ids = expert_ids.reshape(source_count, slot_count)
    onehot = (flat_ids[:, :, None] == jnp.arange(EXPERTS, dtype=jnp.int32)[None, None, :]).astype(jnp.int32)
    before = jnp.cumsum(onehot, axis=1) - onehot
    position = jnp.sum(before * onehot, axis=2).astype(jnp.int32)
    source_index = jnp.broadcast_to(jnp.arange(source_count, dtype=jnp.int32)[:, None], (source_count, slot_count))
    token_index = source_index * MOE_TOK + jnp.arange(slot_count, dtype=jnp.int32)[None, :] // TOPK
    table = jnp.full((source_count, EXPERTS, CAPACITY), MOE_TOKENS, dtype=jnp.int32)
    table = table.at[source_index, flat_ids, position].set(token_index)
    padded = jnp.concatenate([moe_input, jnp.zeros((1, WIDTH), moe_input.dtype)], axis=0)

    def one_expert(inputs):
        expert_table, gate_proj, up_proj, down_proj = inputs
        row_block = padded[expert_table.reshape(-1)]
        return expert_rows(row_block, gate_proj, up_proj, down_proj).reshape(source_count, CAPACITY, WIDTH)

    expert_out = lax.map(one_expert, (jnp.transpose(table, (1, 0, 2)), expert_gate, expert_up, expert_down))
    token_pos = position.reshape(MOE_TOKENS, TOPK)
    token_src = jnp.arange(MOE_TOKENS, dtype=jnp.int32) // MOE_TOK
    running_sum = jnp.zeros((MOE_TOKENS, WIDTH), jnp.float32)
    for slot_number in range(TOPK):
        picked = expert_out[expert_ids[:, slot_number], token_src, token_pos[:, slot_number]]
        running_sum = running_sum + gate_weights[:, slot_number:slot_number + 1] * picked.astype(jnp.float32)
    return attn_out, running_sum.astype(jnp.bfloat16)
```

```python
import jax
import jax.numpy as jnp
from jax import lax
from jax.experimental import pallas as pl
from jax.experimental.pallas import tpu as pltpu
from jax.sharding import Mesh, PartitionSpec as P

WIDTH = 7168
LATENT = 512
KEY_DIM = 576
HEADS = 128
EXPERTS = 32
CTX = 4096
UNITS = 256
TOK = 8
CHIPS = 64
ROWS = CHIPS * TOK
PAY = WIDTH + 128
QK_SCALE = 192.0 ** (-0.5)
FAR_LOW = -1e30
ATT_ROWS = 1024
K_STEP = 512
N_TILE = 896
RET_CUTS = (0, 3584, 7168)
BF = jnp.bfloat16
F32 = jnp.float32
CHIP_AXES = ("z", "x", "y")


def attend_kernel(length_ref, query_ref, cache_ref, out_ref, top_ref, sum_ref, mix_ref):
    step = pl.program_id(0)
    length = length_ref[0]

    @pl.when(step == 0)
    def _():
        top_ref[...] = jnp.full_like(top_ref, FAR_LOW)
        sum_ref[...] = jnp.zeros_like(sum_ref)
        mix_ref[...] = jnp.zeros_like(mix_ref)

    @pl.when(step * ATT_ROWS < length)
    def _():
        rows = cache_ref[...]
        scores = QK_SCALE * lax.dot_general(
            query_ref[0], rows, (((1,), (1,)), ((), ())), preferred_element_type=F32
        )
        place = step * ATT_ROWS + lax.broadcasted_iota(jnp.int32, scores.shape, 1)
        scores = jnp.where(place < length, scores, FAR_LOW)
        top_old = top_ref[...]
        top_new = jnp.maximum(top_old, jnp.max(scores, axis=1, keepdims=True))
        weights = jnp.exp(scores - top_new)
        scale = jnp.exp(top_old - top_new)
        top_ref[...] = top_new
        sum_ref[...] = sum_ref[...] * scale + jnp.sum(weights, axis=1, keepdims=True)
        mix_ref[...] = mix_ref[...] * scale + jnp.dot(
            weights.astype(BF), rows[:, :LATENT], preferred_element_type=F32
        )

    @pl.when(step == pl.num_programs(0) - 1)
    def _():
        out_ref[0] = (mix_ref[...] / sum_ref[...]).astype(BF)


def attend(length, query_rows, cache_latent):
    def cache_block(step, length_ref):
        return jnp.minimum(step, (length_ref[0] - 1) // ATT_ROWS), 0

    return pl.pallas_call(
        attend_kernel,
        grid_spec=pltpu.PrefetchScalarGridSpec(
            num_scalar_prefetch=1,
            grid=(CTX // ATT_ROWS,),
            in_specs=[
                pl.BlockSpec((1, HEADS, KEY_DIM), lambda step, length_ref: (0, 0, 0)),
                pl.BlockSpec((ATT_ROWS, KEY_DIM), cache_block),
            ],
            out_specs=pl.BlockSpec((1, HEADS, LATENT), lambda step, length_ref: (0, 0, 0)),
            scratch_shapes=[
                pltpu.VMEM((HEADS, 1), F32),
                pltpu.VMEM((HEADS, 1), F32),
                pltpu.VMEM((HEADS, LATENT), F32),
            ],
        ),
        out_shape=jax.ShapeDtypeStruct((1, HEADS, LATENT), BF),
        compiler_params=pltpu.CompilerParams(vmem_limit_bytes=24 * 2**20),
        cost_estimate=pl.CostEstimate(
            flops=2 * HEADS * CTX * (KEY_DIM + LATENT),
            bytes_accessed=CTX * KEY_DIM * 2,
            transcendentals=HEADS * CTX,
        ),
        name="attend",
    )(length, query_rows, cache_latent)


def hidden_kernel(x_ref, tail_ref, pick_ref, g0, u0, g1, u1, out_ref, acc_ref):
    step = pl.program_id(0)
    x = x_ref[...]

    @pl.when(step == 0)
    def _():
        acc_ref[...] = jnp.zeros_like(acc_ref)

    for place, weight in enumerate((g0, g1, u0, u1)):
        acc_ref[:, place * UNITS : (place + 1) * UNITS] += jnp.dot(
            x, weight[...], preferred_element_type=F32
        )

    @pl.when(step == pl.num_programs(0) - 1)
    def _():
        share = jnp.dot(tail_ref[...], pick_ref[...], preferred_element_type=F32)
        gate = acc_ref[:, : 2 * UNITS]
        up = acc_ref[:, 2 * UNITS :]
        out_ref[...] = (gate / (1.0 + jnp.exp(-gate)) * up * share).astype(BF)


def hidden_of(payload, pick, gate_own, up_own, gate_other, up_other):
    weight = pl.BlockSpec((K_STEP, UNITS), lambda step: (step, 0))
    return pl.pallas_call(
        hidden_kernel,
        grid=(WIDTH // K_STEP,),
        in_specs=[
            pl.BlockSpec((ROWS, K_STEP), lambda step: (0, step)),
            pl.BlockSpec((ROWS, 128), lambda step: (0, WIDTH // 128)),
            pl.BlockSpec((128, 2 * UNITS), lambda step: (0, 0)),
            weight,
            weight,
            weight,
            weight,
        ],
        out_specs=pl.BlockSpec((ROWS, 2 * UNITS), lambda step: (0, 0)),
        out_shape=jax.ShapeDtypeStruct((ROWS, 2 * UNITS), BF),
        scratch_shapes=[pltpu.VMEM((ROWS, 4 * UNITS), F32)],
        compiler_params=pltpu.CompilerParams(vmem_limit_bytes=32 * 2**20),
        cost_estimate=pl.CostEstimate(
            flops=2 * ROWS * WIDTH * 4 * UNITS,
            bytes_accessed=2 * (ROWS * PAY + 4 * UNITS * WIDTH),
            transcendentals=ROWS * 2 * UNITS,
        ),
        name="hidden",
    )(payload, payload, pick, gate_own, up_own, gate_other, up_other)


def down_kernel(h_ref, d0, d1, out_ref):
    out_ref[...] = (
        jnp.dot(h_ref[:, :UNITS], d0[...], preferred_element_type=F32)
        + jnp.dot(h_ref[:, UNITS:], d1[...], preferred_element_type=F32)
    ).astype(BF)


def down_of(hidden, down_own, down_other, low, high):
    first = low // N_TILE
    weight = pl.BlockSpec((UNITS, N_TILE), lambda step: (0, step + first))
    return pl.pallas_call(
        down_kernel,
        grid=((high - low) // N_TILE,),
        in_specs=[pl.BlockSpec((ROWS, 2 * UNITS), lambda step: (0, 0)), weight, weight],
        out_specs=pl.BlockSpec((ROWS, N_TILE), lambda step: (0, step)),
        out_shape=jax.ShapeDtypeStruct((ROWS, high - low), BF),
        compiler_params=pltpu.CompilerParams(vmem_limit_bytes=24 * 2**20),
        cost_estimate=pl.CostEstimate(
            flops=2 * ROWS * 2 * UNITS * (high - low),
            bytes_accessed=2 * (ROWS * 2 * UNITS + (ROWS + 2 * UNITS) * (high - low)),
            transcendentals=0,
        ),
        name="down",
    )(hidden, down_own, down_other)


def swap(array):
    return lax.ppermute(array, "core", [(0, 1), (1, 0)])


def payload_of(moe_input, expert_ids, gate_weights):
    chosen = expert_ids[:, :, None] == jnp.arange(EXPERTS, dtype=jnp.int32)
    shares = jnp.sum(jnp.where(chosen, gate_weights[:, :, None], 0.0), axis=1)
    high = lax.reduce_precision(shares, 8, 7)
    middle = lax.reduce_precision(shares - high, 8, 7)
    low = lax.reduce_precision(shares - high - middle, 8, 7)
    blank = jnp.zeros((TOK, 128 - 3 * EXPERTS), F32)
    tail = jnp.concatenate([high, middle, low, blank], axis=1).astype(BF)
    return jnp.concatenate([moe_input, tail], axis=1)


def per_device(
    query_rows,
    cache_latent,
    lengths,
    moe_input,
    expert_ids,
    gate_weights,
    expert_gate,
    expert_up,
    expert_down,
):
    chip = (lax.axis_index("z") * 4 + lax.axis_index("x")) * 2
    own = chip + lax.axis_index("core")
    other = chip + 1 - lax.axis_index("core")
    length = lax.dynamic_slice_in_dim(lengths, own * 4 + lax.axis_index("y"), 1)

    payload = payload_of(moe_input, expert_ids, gate_weights)
    arrived = lax.all_gather(payload, CHIP_AXES, axis=0, tiled=True)

    gate_own, up_own, down_own = expert_gate[0], expert_up[0], expert_down[0]
    gate_other, up_other, down_other = swap(gate_own), swap(up_own), swap(down_own)
    attn_out = attend(length, query_rows, cache_latent)

    row = lax.broadcasted_iota(jnp.int32, (128, 2 * UNITS), 0)
    column = lax.broadcasted_iota(jnp.int32, (128, 2 * UNITS), 1)
    wanted = jnp.where(column < UNITS, own, other)
    pick = ((row % EXPERTS == wanted) & (row < 3 * EXPERTS)).astype(BF)

    hidden = hidden_of(arrived, pick, gate_own, up_own, gate_other, up_other)
    sums = []
    for low, high in zip(RET_CUTS, RET_CUTS[1:]):
        made = down_of(hidden, down_own, down_other, low, high).reshape(CHIPS, TOK, high - low)
        back = lax.all_to_all(made, CHIP_AXES, split_axis=0, concat_axis=0, tiled=True)
        sums.append(jnp.sum(back.astype(F32), axis=0).astype(BF))
    return attn_out, jnp.concatenate(sums, axis=1)


def solution(mesh):
    fine = Mesh(mesh.devices.reshape(4, 4, 2, 4), ("z", "x", "core", "y"))
    dp = ("z", "x", "core")
    both = ("z", "x", "core", "y")
    return jax.shard_map(
        per_device,
        mesh=fine,
        in_specs=(
            P(both, None, None),
            P(both, None),
            P(),
            P(both, None),
            P(both, None),
            P(both, None),
            P(dp, None, "y"),
            P(dp, None, "y"),
            P(dp, "y", None),
        ),
        out_specs=(P(both, None, None), P(both, None)),
        check_vma=False,
    )
```

```python
import jax
import jax.numpy as jnp
from jax import lax
from jax.experimental import pallas as pl
from jax.experimental.pallas import tpu as pltpu
from jax.sharding import Mesh, PartitionSpec as P

WIDTH = 7168
LATENT = 512
KEY_DIM = 576
HEADS = 128
EXPERTS = 32
CTX = 4096
UNITS = 256
TOK = 8
CHIPS = 64
ROWS = CHIPS * TOK
PAY = WIDTH + 128
QK_SCALE = 192.0 ** (-0.5)
FAR_LOW = -1e30
ATT_ROWS = 1024
HALF = WIDTH // 2
K_STEP = 512
N_TILE = 512
STEPS = HALF // K_STEP
PART = ROWS // 4
GROUP = ROWS // 16
BF = jnp.bfloat16
F32 = jnp.float32


def attend_kernel(length_ref, query_ref, cache_ref, out_ref, top_ref, sum_ref, mix_ref):
    step = pl.program_id(0)
    length = length_ref[0]

    @pl.when(step == 0)
    def _():
        top_ref[...] = jnp.full_like(top_ref, FAR_LOW)
        sum_ref[...] = jnp.zeros_like(sum_ref)
        mix_ref[...] = jnp.zeros_like(mix_ref)

    @pl.when(step * ATT_ROWS < length)
    def _():
        rows = cache_ref[...]
        scores = QK_SCALE * lax.dot_general(
            query_ref[0], rows, (((1,), (0,)), ((), ())), preferred_element_type=F32
        )
        place = step * ATT_ROWS + lax.broadcasted_iota(jnp.int32, scores.shape, 1)
        scores = jnp.where(place < length, scores, FAR_LOW)
        top_old = top_ref[...]
        top_new = jnp.maximum(top_old, jnp.max(scores, axis=1, keepdims=True))
        weights = jnp.exp(scores - top_new)
        scale = jnp.exp(top_old - top_new)
        top_ref[...] = top_new
        sum_ref[...] = sum_ref[...] * scale + jnp.sum(weights, axis=1, keepdims=True)
        mix_ref[...] = mix_ref[...] * scale + lax.dot_general(
            weights.astype(BF), rows[:LATENT], (((1,), (1,)), ((), ())), preferred_element_type=F32
        )

    @pl.when(step == pl.num_programs(0) - 1)
    def _():
        out_ref[0] = (mix_ref[...] / sum_ref[...]).astype(BF)


def attend(length, query_rows, cache_latent):
    def cache_block(step, length_ref):
        return 0, jnp.minimum(step, (length_ref[0] - 1) // ATT_ROWS)

    return pl.pallas_call(
        attend_kernel,
        grid_spec=pltpu.PrefetchScalarGridSpec(
            num_scalar_prefetch=1,
            grid=(CTX // ATT_ROWS,),
            in_specs=[
                pl.BlockSpec((1, HEADS, KEY_DIM), lambda step, length_ref: (0, 0, 0)),
                pl.BlockSpec((KEY_DIM, ATT_ROWS), cache_block),
            ],
            out_specs=pl.BlockSpec((1, HEADS, LATENT), lambda step, length_ref: (0, 0, 0)),
            scratch_shapes=[
                pltpu.VMEM((HEADS, 1), F32),
                pltpu.VMEM((HEADS, 1), F32),
                pltpu.VMEM((HEADS, LATENT), F32),
            ],
        ),
        out_shape=jax.ShapeDtypeStruct((1, HEADS, LATENT), BF),
        compiler_params=pltpu.CompilerParams(vmem_limit_bytes=24 * 2**20),
        cost_estimate=pl.CostEstimate(
            flops=2 * HEADS * CTX * (KEY_DIM + LATENT),
            bytes_accessed=CTX * KEY_DIM * 2,
            transcendentals=HEADS * CTX,
        ),
        name="attend",
    )(length, query_rows, cache_latent.T)


def dots(xs, weights):
    stacked = xs[0] if len(xs) == 1 else jnp.concatenate(xs, axis=0)
    return [jnp.dot(stacked, weight[...], preferred_element_type=F32) for weight in weights]


def early_kernel(*refs):
    a_refs, b_refs, weights_a, weights_b = refs[:3], refs[3:6], refs[6:10], refs[10:14]
    outs = refs[14:]
    step = pl.program_id(0)

    @pl.when(step == 0)
    def _():
        for out in outs:
            out[...] = jnp.zeros_like(out)

    for blocks, weights, out in ((a_refs, weights_a, outs[0]), (b_refs, weights_b, outs[1])):
        for place, made in enumerate(dots([block[...] for block in blocks], weights)):
            out[:, place * UNITS : (place + 1) * UNITS] += made


def late_kernel(*refs):
    a_ref, b_ref, weights_a, weights_b = refs[0], refs[1], refs[2:6], refs[6:10]
    tails, pick, early_a, early_b = refs[10:14], refs[14], refs[15], refs[16]
    out_a, out_b, last_a, last_b = refs[17:]
    step = pl.program_id(0)

    @pl.when(step == 0)
    def _():
        last_a[...] = jnp.zeros_like(last_a)
        last_b[...] = jnp.zeros_like(last_b)

    for block, weights, last in ((a_ref, weights_a, last_a), (b_ref, weights_b, last_b)):
        for place, made in enumerate(dots([block[...]], weights)):
            last[:, place * UNITS : (place + 1) * UNITS] += made

    @pl.when(step == pl.num_programs(0) - 1)
    def _():
        def group(early, last, outer, inner):
            low = inner * GROUP
            if outer == 3:
                return last[low : low + GROUP, :]
            return early[outer * PART + low : outer * PART + low + GROUP, :]

        for kx in range(4):
            share = jnp.dot(tails[kx][...], pick[...], preferred_element_type=F32)
            for kz in range(4):
                total = group(early_a, last_a, kz, kx) + group(early_b, last_b, kx, kz)
                gate, up = total[:, : 2 * UNITS], total[:, 2 * UNITS :]
                made = gate / (1.0 + jnp.exp(-gate)) * up * share[kz * GROUP : (kz + 1) * GROUP]
                made = made.astype(BF)
                low_a, low_b = (kz * 4 + kx) * GROUP, (kx * 4 + kz) * GROUP
                out_a[low_a : low_a + GROUP, :] = made
                out_b[low_b : low_b + GROUP, :] = made


def hidden_of(parts, pick, weights):
    a_blocks, b_blocks = parts
    block = pl.BlockSpec((PART, K_STEP), lambda step: (0, step))
    first = pl.BlockSpec((K_STEP, UNITS), lambda step: (step, 0))
    second = pl.BlockSpec((K_STEP, UNITS), lambda step: (step + STEPS, 0))
    tail = pl.BlockSpec((PART, 128), lambda step: (0, HALF // 128))

    def whole(rows, columns):
        return pl.BlockSpec((rows, columns), lambda step: (0, 0))

    def cost(blocks):
        return pl.CostEstimate(
            flops=2 * blocks * PART * WIDTH * 4 * UNITS,
            bytes_accessed=2 * (blocks * PART + 4 * UNITS) * WIDTH,
            transcendentals=0,
        )

    sums = jax.ShapeDtypeStruct((3 * PART, 4 * UNITS), F32)
    early_a, early_b = pl.pallas_call(
        early_kernel,
        grid=(STEPS,),
        in_specs=[block] * 6 + [first] * 4 + [second] * 4,
        out_specs=[whole(3 * PART, 4 * UNITS)] * 2,
        out_shape=[sums] * 2,
        compiler_params=pltpu.CompilerParams(vmem_limit_bytes=32 * 2**20),
        cost_estimate=cost(3),
        name="early",
    )(*a_blocks[:3], *b_blocks[:3], *weights, *weights)
    made = jax.ShapeDtypeStruct((ROWS, 2 * UNITS), BF)
    return pl.pallas_call(
        late_kernel,
        grid=(STEPS,),
        in_specs=[block] * 2
        + [first] * 4
        + [second] * 4
        + [tail] * 4
        + [whole(128, 2 * UNITS)]
        + [whole(3 * PART, 4 * UNITS)] * 2,
        out_specs=[whole(ROWS, 2 * UNITS)] * 2,
        out_shape=[made] * 2,
        scratch_shapes=[pltpu.VMEM((PART, 4 * UNITS), F32)] * 2,
        compiler_params=pltpu.CompilerParams(vmem_limit_bytes=32 * 2**20),
        cost_estimate=cost(1),
        name="late",
    )(a_blocks[3], b_blocks[3], *weights, *weights, *b_blocks, pick, early_a, early_b)


def down_kernel(h_a, h_b, d0_a, d1_a, d0_b, d1_b, out_a, out_b):
    for h, d0, d1, out in ((h_a, d0_a, d1_a, out_a), (h_b, d0_b, d1_b, out_b)):
        out[...] = (
            jnp.dot(h[:, :UNITS], d0[...], preferred_element_type=F32)
            + jnp.dot(h[:, UNITS:], d1[...], preferred_element_type=F32)
        ).astype(BF)


def down_of(hidden, downs, index):
    rows = pl.BlockSpec((PART, 2 * UNITS), lambda step: (index, 0))
    first = pl.BlockSpec((UNITS, N_TILE), lambda step: (0, step))
    second = pl.BlockSpec((UNITS, N_TILE), lambda step: (0, step + HALF // N_TILE))
    return pl.pallas_call(
        down_kernel,
        grid=(HALF // N_TILE,),
        in_specs=[rows, rows, first, first, second, second],
        out_specs=[pl.BlockSpec((PART, N_TILE), lambda step: (0, step))] * 2,
        out_shape=[jax.ShapeDtypeStruct((PART, HALF), BF)] * 2,
        compiler_params=pltpu.CompilerParams(vmem_limit_bytes=24 * 2**20),
        cost_estimate=pl.CostEstimate(
            flops=2 * PART * 2 * UNITS * WIDTH,
            bytes_accessed=2 * (PART + 2 * UNITS) * WIDTH,
            transcendentals=0,
        ),
        name="down",
    )(*hidden, *downs, *downs)


def swap(array):
    return lax.ppermute(array, "core", [(0, 1), (1, 0)])


def move(array, axis, way):
    names = ("core", axis) if axis == "y" else (axis, "core")

    def flat(core, place):
        return core * 4 + place if axis == "y" else place * 2 + core

    pairs = [
        (flat(core, place), flat(core, (place + (way if core == 0 else -way)) % 4))
        for core in range(2)
        for place in range(4)
    ]
    return lax.ppermute(array, names, pairs)


def gather_stage(parts, axes):
    first = [move(part, axis, 1) for part, axis in zip(parts, axes)]
    second = [move(part, axis, -1) for part, axis in zip(parts, axes)]
    third = [move(part, axis, 1) for part, axis in zip(first, axes)]
    return [list(blocks) for blocks in zip(parts, first, second, third)]


def joined(blocks):
    return jnp.concatenate(blocks, axis=0)


def added(*terms):
    total = terms[0].astype(F32)
    for term in terms[1:]:
        total = total + term.astype(F32)
    return total.astype(BF)


def reduce_stage(parts, axes):
    far = [move(blocks[3], axis, -1) for blocks, axis in zip(parts, axes)]
    near = [move(blocks[2], axis, 1) for blocks, axis in zip(parts, axes)]
    last = [
        move(added(blocks[1], relayed), axis, -1)
        for blocks, relayed, axis in zip(parts, far, axes)
    ]
    return [added(blocks[0], n, l) for blocks, n, l in zip(parts, near, last)]


def quarters(array):
    return jnp.split(array, 4, axis=0)


def payload_of(moe_input, expert_ids, gate_weights):
    chosen = expert_ids[:, :, None] == jnp.arange(EXPERTS, dtype=jnp.int32)
    shares = jnp.sum(jnp.where(chosen, gate_weights[:, :, None], 0.0), axis=1)
    high = lax.reduce_precision(shares, 8, 7)
    middle = lax.reduce_precision(shares - high, 8, 7)
    low = lax.reduce_precision(shares - high - middle, 8, 7)
    blank = jnp.zeros((TOK, 128 - 3 * EXPERTS), F32)
    tail = jnp.concatenate([high, middle, low, blank], axis=1).astype(BF)
    return jnp.concatenate([moe_input, tail], axis=1)


def per_device(
    query_rows,
    cache_latent,
    lengths,
    moe_input,
    expert_ids,
    gate_weights,
    expert_gate,
    expert_up,
    expert_down,
):
    chip = (lax.axis_index("z") * 4 + lax.axis_index("x")) * 2
    own = chip + lax.axis_index("core")
    other = chip + 1 - lax.axis_index("core")
    length = lax.dynamic_slice_in_dim(lengths, own * 4 + lax.axis_index("y"), 1)

    payload = payload_of(moe_input, expert_ids, gate_weights)
    column = joined(gather_stage([payload], ["y"])[0])
    plane = gather_stage([column[:, :HALF], column[:, HALF:]], ["x", "z"])
    parts = gather_stage([joined(blocks) for blocks in plane], ["z", "x"])

    gate_own, up_own, down_own = expert_gate[0], expert_up[0], expert_down[0]
    gate_other, up_other, down_other = swap(gate_own), swap(up_own), swap(down_own)
    attn_out = attend(length, query_rows, cache_latent)

    row = lax.broadcasted_iota(jnp.int32, (128, 2 * UNITS), 0)
    lane = lax.broadcasted_iota(jnp.int32, (128, 2 * UNITS), 1)
    wanted = jnp.where(lane < UNITS, own, other)
    pick = ((row % EXPERTS == wanted) & (row < 3 * EXPERTS)).astype(BF)

    hidden = hidden_of(parts, pick, (gate_own, gate_other, up_own, up_other))
    made = [None] * 4
    for index in (3, 2, 1, 0):
        made[index] = down_of(hidden, (down_own, down_other), index)
    sums = reduce_stage([[pair[0] for pair in made], [pair[1] for pair in made]], ["z", "x"])
    sums = reduce_stage([quarters(part) for part in sums], ["x", "z"])
    moe_out = reduce_stage([quarters(jnp.concatenate(sums, axis=1))], ["y"])[0]
    return attn_out, moe_out


def solution(mesh):
    fine = Mesh(mesh.devices.reshape(4, 4, 2, 4), ("z", "x", "core", "y"))
    dp = ("z", "x", "core")
    both = ("z", "x", "core", "y")
    return jax.shard_map(
        per_device,
        mesh=fine,
        in_specs=(
            P(both, None, None),
            P(both, None),
            P(),
            P(both, None),
            P(both, None),
            P(both, None),
            P(dp, None, "y"),
            P(dp, None, "y"),
            P(dp, "y", None),
        ),
        out_specs=(P(both, None, None), P(both, None)),
        check_vma=False,
    )
```

```python
import jax
import jax.numpy as jnp
from jax import lax
from jax.experimental import pallas as pl
from jax.experimental.pallas import tpu as pltpu
from jax.sharding import Mesh, PartitionSpec as P

WIDTH = 7168
LATENT = 512
KEY_DIM = 576
HEADS = 128
EXPERTS = 32
CTX = 4096
UNITS = 256
TOK = 8
CHIPS = 64
ROWS = CHIPS * TOK
PAY = WIDTH + 128
QK_SCALE = 192.0 ** (-0.5)
FAR_LOW = -1e30
ATT_ROWS = 1024
HALF = WIDTH // 2
K_STEP = 512
N_TILE = 896
VMEM_LIMIT = 48 * 2**20
STEPS = HALF // K_STEP
PART = ROWS // 4
GROUP = ROWS // 16
BF = jnp.bfloat16
F32 = jnp.float32


def attend_kernel(length_ref, query_ref, cache_ref, out_ref, top_ref, sum_ref, mix_ref):
    step = pl.program_id(0)
    length = length_ref[0]

    @pl.when(step == 0)
    def _():
        top_ref[...] = jnp.full_like(top_ref, FAR_LOW)
        sum_ref[...] = jnp.zeros_like(sum_ref)
        mix_ref[...] = jnp.zeros_like(mix_ref)

    @pl.when(step * ATT_ROWS < length)
    def _():
        rows = cache_ref[...]
        scores = QK_SCALE * lax.dot_general(
            query_ref[0], rows, (((1,), (0,)), ((), ())), preferred_element_type=F32
        )
        place = step * ATT_ROWS + lax.broadcasted_iota(jnp.int32, scores.shape, 1)
        scores = jnp.where(place < length, scores, FAR_LOW)
        top_old = top_ref[...]
        top_new = jnp.maximum(top_old, jnp.max(scores, axis=1, keepdims=True))
        weights = jnp.exp(scores - top_new)
        scale = jnp.exp(top_old - top_new)
        top_ref[...] = top_new
        sum_ref[...] = sum_ref[...] * scale + jnp.sum(weights, axis=1, keepdims=True)
        mix_ref[...] = mix_ref[...] * scale + lax.dot_general(
            weights.astype(BF), rows[:LATENT], (((1,), (1,)), ((), ())), preferred_element_type=F32
        )

    @pl.when(step == pl.num_programs(0) - 1)
    def _():
        out_ref[0] = (mix_ref[...] / sum_ref[...]).astype(BF)


def attend(length, query_rows, cache_latent):
    def cache_block(step, length_ref):
        return 0, jnp.minimum(step, (length_ref[0] - 1) // ATT_ROWS)

    return pl.pallas_call(
        attend_kernel,
        grid_spec=pltpu.PrefetchScalarGridSpec(
            num_scalar_prefetch=1,
            grid=(CTX // ATT_ROWS,),
            in_specs=[
                pl.BlockSpec((1, HEADS, KEY_DIM), lambda step, length_ref: (0, 0, 0)),
                pl.BlockSpec((KEY_DIM, ATT_ROWS), cache_block),
            ],
            out_specs=pl.BlockSpec((1, HEADS, LATENT), lambda step, length_ref: (0, 0, 0)),
            scratch_shapes=[
                pltpu.VMEM((HEADS, 1), F32),
                pltpu.VMEM((HEADS, 1), F32),
                pltpu.VMEM((HEADS, LATENT), F32),
            ],
        ),
        out_shape=jax.ShapeDtypeStruct((1, HEADS, LATENT), BF),
        compiler_params=pltpu.CompilerParams(vmem_limit_bytes=24 * 2**20),
        cost_estimate=pl.CostEstimate(
            flops=2 * HEADS * CTX * (KEY_DIM + LATENT),
            bytes_accessed=CTX * KEY_DIM * 2,
            transcendentals=HEADS * CTX,
        ),
        name="attend",
    )(length, query_rows, cache_latent.T)


def dots(xs, weights):
    stacked = xs[0] if len(xs) == 1 else jnp.concatenate(xs, axis=0)
    return [jnp.dot(stacked, weight[...], preferred_element_type=F32) for weight in weights]


def early_kernel(*refs):
    a_refs, b_refs, weights_a, weights_b = refs[:3], refs[3:6], refs[6:10], refs[10:14]
    outs = refs[14:]
    step = pl.program_id(0)

    @pl.when(step == 0)
    def _():
        for out in outs:
            out[...] = jnp.zeros_like(out)

    for blocks, weights, out in ((a_refs, weights_a, outs[0]), (b_refs, weights_b, outs[1])):
        for place, made in enumerate(dots([block[...] for block in blocks], weights)):
            out[:, place * UNITS : (place + 1) * UNITS] += made


def late_kernel(*refs):
    a_ref, b_ref, weights_a, weights_b = refs[0], refs[1], refs[2:6], refs[6:10]
    tails, pick, sources = refs[10:14], refs[14], refs[15:17]
    out_a, out_b, last_a, last_b, early_a, early_b, arrival = refs[17:]
    step = pl.program_id(0)
    fetches = [
        pltpu.make_async_copy(source, kept, arrival.at[place])
        for place, (source, kept) in enumerate(zip(sources, (early_a, early_b)))
    ]

    @pl.when(step == 0)
    def _():
        for fetch in fetches:
            fetch.start()
        last_a[...] = jnp.zeros_like(last_a)
        last_b[...] = jnp.zeros_like(last_b)

    for block, weights, last in ((a_ref, weights_a, last_a), (b_ref, weights_b, last_b)):
        for place, made in enumerate(dots([block[...]], weights)):
            last[:, place * UNITS : (place + 1) * UNITS] += made

    @pl.when(step == pl.num_programs(0) - 1)
    def _():
        for fetch in fetches:
            fetch.wait()

        def group(early, last, outer, inner):
            low = inner * GROUP
            if outer == 3:
                return last[low : low + GROUP, :]
            return early[outer * PART + low : outer * PART + low + GROUP, :]

        for kx in range(4):
            share = jnp.dot(tails[kx][...], pick[...], preferred_element_type=F32)
            for kz in range(4):
                total = group(early_a, last_a, kz, kx) + group(early_b, last_b, kx, kz)
                gate, up = total[:, : 2 * UNITS], total[:, 2 * UNITS :]
                made = gate / (1.0 + jnp.exp(-gate)) * up * share[kz * GROUP : (kz + 1) * GROUP]
                made = made.astype(BF)
                low_a, low_b = (kz * 4 + kx) * GROUP, (kx * 4 + kz) * GROUP
                out_a[low_a : low_a + GROUP, :] = made
                out_b[low_b : low_b + GROUP, :] = made


def hidden_of(parts, pick, weights):
    a_blocks, b_blocks = parts
    block = pl.BlockSpec((PART, K_STEP), lambda step: (0, step))
    first = pl.BlockSpec((K_STEP, UNITS), lambda step: (step, 0))
    second = pl.BlockSpec((K_STEP, UNITS), lambda step: (step + STEPS, 0))
    tail = pl.BlockSpec((PART, 128), lambda step: (0, HALF // 128))

    def whole(rows, columns):
        return pl.BlockSpec((rows, columns), lambda step: (0, 0))

    def cost(blocks):
        return pl.CostEstimate(
            flops=2 * blocks * PART * WIDTH * 4 * UNITS,
            bytes_accessed=2 * (blocks * PART + 4 * UNITS) * WIDTH,
            transcendentals=0,
        )

    sums = jax.ShapeDtypeStruct((3 * PART, 4 * UNITS), F32)
    early_a, early_b = pl.pallas_call(
        early_kernel,
        grid=(STEPS,),
        in_specs=[block] * 6 + [first] * 4 + [second] * 4,
        out_specs=[whole(3 * PART, 4 * UNITS)] * 2,
        out_shape=[sums] * 2,
        compiler_params=pltpu.CompilerParams(vmem_limit_bytes=VMEM_LIMIT),
        cost_estimate=cost(3),
        name="early",
    )(*a_blocks[:3], *b_blocks[:3], *weights, *weights)
    made = jax.ShapeDtypeStruct((ROWS, 2 * UNITS), BF)
    return pl.pallas_call(
        late_kernel,
        grid=(STEPS,),
        in_specs=[block] * 2
        + [first] * 4
        + [second] * 4
        + [tail] * 4
        + [whole(128, 2 * UNITS)]
        + [pl.BlockSpec(memory_space=pl.ANY)] * 2,
        out_specs=[whole(ROWS, 2 * UNITS)] * 2,
        out_shape=[made] * 2,
        scratch_shapes=[pltpu.VMEM((PART, 4 * UNITS), F32)] * 2
        + [pltpu.VMEM((3 * PART, 4 * UNITS), F32)] * 2
        + [pltpu.SemaphoreType.DMA((2,))],
        compiler_params=pltpu.CompilerParams(vmem_limit_bytes=VMEM_LIMIT),
        cost_estimate=cost(1),
        name="late",
    )(a_blocks[3], b_blocks[3], *weights, *weights, *b_blocks, pick, early_a, early_b)


def down_kernel(h, d0, d1, *outs):
    made = (
        jnp.dot(h[:, :UNITS], d0[...], preferred_element_type=F32)
        + jnp.dot(h[:, UNITS:], d1[...], preferred_element_type=F32)
    ).astype(BF)
    for place, out in enumerate(outs):
        out[...] = made[place * PART : (place + 1) * PART]


def down_of(hidden, downs, half):
    first = half * (HALF // N_TILE)
    weight = pl.BlockSpec((UNITS, N_TILE), lambda step: (0, step + first))
    return pl.pallas_call(
        down_kernel,
        grid=(HALF // N_TILE,),
        in_specs=[pl.BlockSpec((ROWS, 2 * UNITS), lambda step: (0, 0)), weight, weight],
        out_specs=[pl.BlockSpec((PART, N_TILE), lambda step: (0, step))] * 4,
        out_shape=[jax.ShapeDtypeStruct((PART, HALF), BF)] * 4,
        compiler_params=pltpu.CompilerParams(vmem_limit_bytes=24 * 2**20),
        cost_estimate=pl.CostEstimate(
            flops=2 * ROWS * 2 * UNITS * HALF,
            bytes_accessed=2 * (ROWS + 2 * UNITS) * HALF,
            transcendentals=0,
        ),
        name="down",
    )(hidden, *downs)


def swap(array):
    return lax.ppermute(array, "core", [(0, 1), (1, 0)])


def move(array, axis, way):
    names = ("core", axis) if axis == "y" else (axis, "core")

    def flat(core, place):
        return core * 4 + place if axis == "y" else place * 2 + core

    pairs = [
        (flat(core, place), flat(core, (place + (way if core == 0 else -way)) % 4))
        for core in range(2)
        for place in range(4)
    ]
    return lax.ppermute(array, names, pairs)


def gather_stage(parts, axes):
    return [
        [part, move(part, axis, 1), move(part, axis, -1), move(part, axis, 2)]
        for part, axis in zip(parts, axes)
    ]


def joined(blocks):
    return jnp.concatenate(blocks, axis=0)


def added(*terms):
    total = terms[0].astype(F32)
    for term in terms[1:]:
        total = total + term.astype(F32)
    return total.astype(BF)


def reduce_stage(parts, axes, relay):
    if not relay:
        far = [move(blocks[3], axis, 2) for blocks, axis in zip(parts, axes)]
        near = [move(blocks[2], axis, 1) for blocks, axis in zip(parts, axes)]
        last = [move(blocks[1], axis, -1) for blocks, axis in zip(parts, axes)]
        return [
            added(blocks[0], n, l, f) for blocks, n, l, f in zip(parts, near, last, far)
        ]
    far = [move(blocks[3], axis, -1) for blocks, axis in zip(parts, axes)]
    near = [move(blocks[2], axis, 1) for blocks, axis in zip(parts, axes)]
    last = [
        move(added(blocks[1], relayed), axis, -1)
        for blocks, relayed, axis in zip(parts, far, axes)
    ]
    return [added(blocks[0], n, l) for blocks, n, l in zip(parts, near, last)]


def quarters(array):
    return jnp.split(array, 4, axis=0)


def payload_of(moe_input, expert_ids, gate_weights):
    chosen = expert_ids[:, :, None] == jnp.arange(EXPERTS, dtype=jnp.int32)
    shares = jnp.sum(jnp.where(chosen, gate_weights[:, :, None], 0.0), axis=1)
    high = lax.reduce_precision(shares, 8, 7)
    middle = lax.reduce_precision(shares - high, 8, 7)
    low = lax.reduce_precision(shares - high - middle, 8, 7)
    blank = jnp.zeros((TOK, 128 - 3 * EXPERTS), F32)
    tail = jnp.concatenate([high, middle, low, blank], axis=1).astype(BF)
    return jnp.concatenate([moe_input, tail], axis=1)


def per_device(
    query_rows,
    cache_latent,
    lengths,
    moe_input,
    expert_ids,
    gate_weights,
    expert_gate,
    expert_up,
    expert_down,
):
    chip = (lax.axis_index("z") * 4 + lax.axis_index("x")) * 2
    own = chip + lax.axis_index("core")
    other = chip + 1 - lax.axis_index("core")
    length = lax.dynamic_slice_in_dim(lengths, own * 4 + lax.axis_index("y"), 1)

    payload = payload_of(moe_input, expert_ids, gate_weights)
    gate_own, up_own, down_own = expert_gate[0], expert_up[0], expert_down[0]
    column = joined(gather_stage([payload], ["y"])[0])
    column, gate_other, up_other = lax.optimization_barrier(
        (column, swap(gate_own), swap(up_own))
    )
    plane = gather_stage([column[:, :HALF], column[:, HALF:]], ["x", "z"])
    both = [joined(blocks) for blocks in plane]
    both, query_rows, down_own = lax.optimization_barrier((both, query_rows, down_own))
    down_other = swap(down_own)
    first = [move(part, axis, 1) for part, axis in zip(both, "zx")]
    second = [move(part, axis, -1) for part, axis in zip(both, "zx")]
    attn_out = attend(length, query_rows, cache_latent)
    first, attn_out = lax.optimization_barrier((first, attn_out))
    third = [move(part, axis, 1) for part, axis in zip(first, "zx")]
    parts = [list(blocks) for blocks in zip(both, first, second, third)]

    row = lax.broadcasted_iota(jnp.int32, (128, 2 * UNITS), 0)
    lane = lax.broadcasted_iota(jnp.int32, (128, 2 * UNITS), 1)
    wanted = jnp.where(lane < UNITS, own, other)
    pick = ((row % EXPERTS == wanted) & (row < 3 * EXPERTS)).astype(BF)

    hidden = hidden_of(parts, pick, (gate_own, gate_other, up_own, up_other))
    made = [down_of(hidden[half], (down_own, down_other), half) for half in range(2)]
    sums = reduce_stage(made, ["z", "x"], True)
    sums = reduce_stage([quarters(part) for part in sums], ["x", "z"], True)
    moe_out = reduce_stage([quarters(jnp.concatenate(sums, axis=1))], ["y"], False)[0]
    return attn_out, moe_out


def solution(mesh):
    fine = Mesh(mesh.devices.reshape(4, 4, 2, 4), ("z", "x", "core", "y"))
    dp = ("z", "x", "core")
    both = ("z", "x", "core", "y")
    return jax.shard_map(
        per_device,
        mesh=fine,
        in_specs=(
            P(both, None, None),
            P(both, None),
            P(),
            P(both, None),
            P(both, None),
            P(both, None),
            P(dp, None, "y"),
            P(dp, None, "y"),
            P(dp, "y", None),
        ),
        out_specs=(P(both, None, None), P(both, None)),
        check_vma=False,
    )
```

```python
import functools

import jax
import jax.numpy as jnp
from jax import lax
from jax.experimental import pallas as pl
from jax.experimental.pallas import tpu as pltpu
from jax.sharding import Mesh, PartitionSpec as P

WIDTH = 7168
LATENT = 512
KEY_DIM = 576
HEADS = 128
EXPERTS = 32
CTX = 4096
UNITS = 256
TOK = 8
CHIPS = 64
ROWS = CHIPS * TOK
PAY = WIDTH + 128
QK_SCALE = 192.0 ** (-0.5)
FAR_LOW = -1e30
ATT_ROWS = 1024
HALF = WIDTH // 2
K_STEP = 512
RETURN = (3584, 3584)
N_TILE = 896
VMEM_LIMIT = 8 * 2**20
STEPS = HALF // K_STEP
D_STEP = WIDTH // STEPS
PART = ROWS // 4
GROUP = ROWS // 16
BF = jnp.bfloat16
F32 = jnp.float32


def attend_kernel(length_ref, query_ref, cache_ref, out_ref, top_ref, sum_ref, mix_ref):
    step = pl.program_id(0)
    length = length_ref[0]

    @pl.when(step == 0)
    def _():
        top_ref[...] = jnp.full_like(top_ref, FAR_LOW)
        sum_ref[...] = jnp.zeros_like(sum_ref)
        mix_ref[...] = jnp.zeros_like(mix_ref)

    @pl.when(step * ATT_ROWS < length)
    def _():
        rows = cache_ref[...]
        scores = QK_SCALE * lax.dot_general(
            query_ref[0], rows, (((1,), (0,)), ((), ())), preferred_element_type=F32
        )
        place = step * ATT_ROWS + lax.broadcasted_iota(jnp.int32, scores.shape, 1)
        scores = jnp.where(place < length, scores, FAR_LOW)
        top_old = top_ref[...]
        top_new = jnp.maximum(top_old, jnp.max(scores, axis=1, keepdims=True))
        weights = jnp.exp(scores - top_new)
        scale = jnp.exp(top_old - top_new)
        top_ref[...] = top_new
        sum_ref[...] = sum_ref[...] * scale + jnp.sum(weights, axis=1, keepdims=True)
        mix_ref[...] = mix_ref[...] * scale + lax.dot_general(
            weights.astype(BF), rows[:LATENT], (((1,), (1,)), ((), ())), preferred_element_type=F32
        )

    @pl.when(step == pl.num_programs(0) - 1)
    def _():
        out_ref[0] = (mix_ref[...] / sum_ref[...]).astype(BF)


def attend(length, query_rows, cache_latent):
    def cache_block(step, length_ref):
        return 0, jnp.minimum(step, (length_ref[0] - 1) // ATT_ROWS)

    return pl.pallas_call(
        attend_kernel,
        grid_spec=pltpu.PrefetchScalarGridSpec(
            num_scalar_prefetch=1,
            grid=(CTX // ATT_ROWS,),
            in_specs=[
                pl.BlockSpec((1, HEADS, KEY_DIM), lambda step, length_ref: (0, 0, 0)),
                pl.BlockSpec((KEY_DIM, ATT_ROWS), cache_block),
            ],
            out_specs=pl.BlockSpec((1, HEADS, LATENT), lambda step, length_ref: (0, 0, 0)),
            scratch_shapes=[
                pltpu.VMEM((HEADS, 1), F32),
                pltpu.VMEM((HEADS, 1), F32),
                pltpu.VMEM((HEADS, LATENT), F32),
            ],
        ),
        out_shape=jax.ShapeDtypeStruct((1, HEADS, LATENT), BF),
        compiler_params=pltpu.CompilerParams(vmem_limit_bytes=VMEM_LIMIT),
        cost_estimate=pl.CostEstimate(
            flops=2 * HEADS * CTX * (KEY_DIM + LATENT),
            bytes_accessed=CTX * KEY_DIM * 2,
            transcendentals=HEADS * CTX,
        ),
        name="attend",
    )(length, query_rows, cache_latent.T)


def own_kernel(*refs):
    a_ref, b_ref, weights_a, weights_b, d_own, d_other = *refs[:2], refs[2:6], refs[6:10], *refs[10:12]
    out_a, out_b, held, down = refs[12:]
    step = pl.program_id(0)

    @pl.when(step == 0)
    def _():
        out_a[...] = jnp.zeros_like(out_a)
        out_b[...] = jnp.zeros_like(out_b)

    for block, weights, out, start in ((a_ref, weights_a, out_a, 0), (b_ref, weights_b, out_b, HALF)):
        rows = pl.ds(pl.multiple_of(start + step * K_STEP, K_STEP), K_STEP)
        for place, weight in enumerate(weights):
            lanes = slice(place * UNITS, (place + 1) * UNITS)
            value = weight[...]
            held[rows, lanes] = value
            out[:, lanes] += jnp.dot(block[...], value, preferred_element_type=F32)
    columns = pl.ds(pl.multiple_of(step * D_STEP, D_STEP), D_STEP)
    down[:UNITS, columns] = d_own[...]
    down[UNITS:, columns] = d_other[...]


def own_part(a_block, b_block, weights, downs):
    block = pl.BlockSpec((PART, K_STEP), lambda step: (0, step))
    first = pl.BlockSpec((K_STEP, UNITS), lambda step: (step, 0))
    second = pl.BlockSpec((K_STEP, UNITS), lambda step: (step + STEPS, 0))
    down = pl.BlockSpec((UNITS, D_STEP), lambda step: (0, step))
    sums = pl.BlockSpec((PART, 4 * UNITS), lambda step: (0, 0))
    return pl.pallas_call(
        own_kernel,
        grid=(STEPS,),
        in_specs=[block] * 2 + [first] * 4 + [second] * 4 + [down] * 2,
        out_specs=[sums] * 2 + [pl.BlockSpec(memory_space=pltpu.VMEM)] * 2,
        out_shape=[jax.ShapeDtypeStruct((PART, 4 * UNITS), F32)] * 2
        + [pltpu.VMEM((WIDTH, 4 * UNITS), BF), pltpu.VMEM((2 * UNITS, WIDTH), BF)],
        compiler_params=pltpu.CompilerParams(vmem_limit_bytes=VMEM_LIMIT),
        cost_estimate=pl.CostEstimate(
            flops=2 * PART * WIDTH * 4 * UNITS,
            bytes_accessed=2 * (PART + 6 * UNITS) * WIDTH,
            transcendentals=0,
        ),
        name="own",
    )(a_block, b_block, *weights, *weights, *downs)


def on_chip(kernel, name, operands, shapes, flops, aliases=()):
    spec = pl.BlockSpec(memory_space=pltpu.VMEM)
    return pl.pallas_call(
        kernel,
        in_specs=[spec] * len(operands),
        out_specs=[spec] * len(shapes),
        out_shape=[pltpu.VMEM(*shape) for shape in shapes],
        compiler_params=pltpu.CompilerParams(vmem_limit_bytes=VMEM_LIMIT),
        cost_estimate=pl.CostEstimate(flops=flops, bytes_accessed=0, transcendentals=0),
        input_output_aliases=dict(aliases),
        name=name,
    )(*operands)


def early_kernel(a1, a2, b1, b2, held, out_a, out_b, _):
    for blocks, out, start in (((a1, a2), out_a, 0), ((b1, b2), out_b, HALF)):
        stacked = jnp.concatenate([block[:, :HALF] for block in blocks], axis=0)
        out[...] = jnp.dot(stacked, held[start : start + HALF], preferred_element_type=F32)


def send_blocks(hidden, down, low, outs):
    width = outs[0].shape[1]
    for start in range(0, width, N_TILE):
        made = jnp.dot(
            hidden[...], down[:, low + start : low + start + N_TILE], preferred_element_type=F32
        ).astype(BF)
        for place, out in enumerate(outs):
            out[:, start : start + N_TILE] = made[place * PART : (place + 1) * PART]


def late_kernel(a3, b0, b1, b2, b3, held, pick, own_a, own_b, early_a, early_b, out_a, out_b):
    last_a = jnp.dot(a3[...], held[:HALF], preferred_element_type=F32)
    last_b = jnp.dot(b3[:, :HALF], held[HALF:], preferred_element_type=F32)

    def group(own, early, last, outer, inner):
        low = inner * GROUP
        if outer == 0:
            return own[low : low + GROUP]
        if outer == 3:
            return last[low : low + GROUP]
        low = low + (outer - 1) * PART
        return early[low : low + GROUP]

    for kx, tail in enumerate((b0, b1, b2, b3)):
        share = jnp.dot(tail[:, HALF:], pick[...], preferred_element_type=F32)
        for kz in range(4):
            total = group(own_a, early_a, last_a, kz, kx) + group(own_b, early_b, last_b, kx, kz)
            gate, up = total[:, : 2 * UNITS], total[:, 2 * UNITS :]
            made = gate / (1.0 + jnp.exp(-gate)) * up * share[kz * GROUP : (kz + 1) * GROUP]
            made = made.astype(BF)
            low_a, low_b = (kz * 4 + kx) * GROUP, (kx * 4 + kz) * GROUP
            out_a[low_a : low_a + GROUP, :] = made
            out_b[low_b : low_b + GROUP, :] = made


def down_kernel(low, hidden, down, *outs):
    send_blocks(hidden, down, low, outs)


def sent_blocks(parts, own_sums, held, down, pick):
    a_blocks, b_blocks = parts
    sums = ((2 * PART, 4 * UNITS), F32)
    *early_sums, held = on_chip(
        early_kernel,
        "early",
        (*a_blocks[1:3], *b_blocks[1:3], held),
        (sums, sums, ((WIDTH, 4 * UNITS), BF)),
        2 * 2 * PART * WIDTH * 4 * UNITS,
        {4: 2},
    )
    made = ((ROWS, 2 * UNITS), BF)
    halves = on_chip(
        late_kernel,
        "late",
        (a_blocks[3], *b_blocks, held, pick, *own_sums, *early_sums),
        (made, made),
        2 * PART * WIDTH * 4 * UNITS,
    )
    def half(place, hidden):
        return on_chip(
            functools.partial(down_kernel, place * RETURN[0]),
            "down",
            (hidden, down),
            [((PART, RETURN[place]), BF)] * 4,
            2 * ROWS * 2 * UNITS * RETURN[place],
        )

    first, hidden = lax.optimization_barrier((half(0, halves[0]), halves[1]))
    return [first, half(1, hidden)]


def swap(array):
    return lax.ppermute(array, "core", [(0, 1), (1, 0)])


def move(array, axis, way):
    names = ("core", axis) if axis == "y" else (axis, "core")

    def flat(core, place):
        return core * 4 + place if axis == "y" else place * 2 + core

    pairs = [
        (flat(core, place), flat(core, (place + (way if core == 0 else -way)) % 4))
        for core in range(2)
        for place in range(4)
    ]
    return lax.ppermute(array, names, pairs)


def gather_stage(parts, axes):
    return [
        [part, move(part, axis, 1), move(part, axis, -1), move(part, axis, 2)]
        for part, axis in zip(parts, axes)
    ]


def joined(blocks):
    return jnp.concatenate(blocks, axis=0)


def added(*terms):
    total = terms[0].astype(F32)
    for term in terms[1:]:
        total = total + term.astype(F32)
    return total.astype(BF)


def reduce_stage(parts, axes, relay):
    if not relay:
        far = [move(blocks[3], axis, 2) for blocks, axis in zip(parts, axes)]
        near = [move(blocks[2], axis, 1) for blocks, axis in zip(parts, axes)]
        last = [move(blocks[1], axis, -1) for blocks, axis in zip(parts, axes)]
        return [
            added(blocks[0], n, l, f) for blocks, n, l, f in zip(parts, near, last, far)
        ]
    far = [move(blocks[3], axis, -1) for blocks, axis in zip(parts, axes)]
    near = [move(blocks[2], axis, 1) for blocks, axis in zip(parts, axes)]
    last = [
        move(added(blocks[1], relayed), axis, -1)
        for blocks, relayed, axis in zip(parts, far, axes)
    ]
    return [added(blocks[0], n, l) for blocks, n, l in zip(parts, near, last)]


def quarters(array):
    return jnp.split(array, 4, axis=0)


def payload_of(moe_input, expert_ids, gate_weights):
    chosen = expert_ids[:, :, None] == jnp.arange(EXPERTS, dtype=jnp.int32)
    shares = jnp.sum(jnp.where(chosen, gate_weights[:, :, None], 0.0), axis=1)
    high = lax.reduce_precision(shares, 8, 7)
    middle = lax.reduce_precision(shares - high, 8, 7)
    low = lax.reduce_precision(shares - high - middle, 8, 7)
    blank = jnp.zeros((TOK, 128 - 3 * EXPERTS), F32)
    tail = jnp.concatenate([high, middle, low, blank], axis=1).astype(BF)
    return jnp.concatenate([moe_input, tail], axis=1)


def per_device(
    query_rows,
    cache_latent,
    lengths,
    moe_input,
    expert_ids,
    gate_weights,
    expert_gate,
    expert_up,
    expert_down,
):
    chip = (lax.axis_index("z") * 4 + lax.axis_index("x")) * 2
    own = chip + lax.axis_index("core")
    other = chip + 1 - lax.axis_index("core")
    length = lax.dynamic_slice_in_dim(lengths, own * 4 + lax.axis_index("y"), 1)

    row = lax.broadcasted_iota(jnp.int32, (128, 2 * UNITS), 0)
    lane = lax.broadcasted_iota(jnp.int32, (128, 2 * UNITS), 1)
    wanted = jnp.where(lane < UNITS, own, other)
    pick = ((row % EXPERTS == wanted) & (row < 3 * EXPERTS)).astype(BF)

    payload = payload_of(moe_input, expert_ids, gate_weights)
    gate_own, up_own, down_own = expert_gate[0], expert_up[0], expert_down[0]
    column = joined(gather_stage([payload], ["y"])[0])
    column, gate_other, up_other = lax.optimization_barrier(
        (column, swap(gate_own), swap(up_own))
    )
    plane = gather_stage([column[:, :HALF], column[:, HALF:]], ["x", "z"])
    both = [joined(blocks) for blocks in plane]
    both, query_rows, down_own, pick, length = lax.optimization_barrier(
        (both, query_rows, down_own, pick, length)
    )
    down_other = swap(down_own)
    first = [move(part, axis, 1) for part, axis in zip(both, "zx")]
    second = [move(part, axis, -1) for part, axis in zip(both, "zx")]
    attn_out = attend(length, query_rows, cache_latent)
    *own_sums, held, down = own_part(
        both[0], both[1], (gate_own, gate_other, up_own, up_other), (down_own, down_other)
    )
    first, attn_out, own_sums = lax.optimization_barrier((first, attn_out, own_sums))
    third = [move(part, axis, 1) for part, axis in zip(first, "zx")]
    parts = [list(blocks) for blocks in zip(both, first, second, third)]

    made = sent_blocks(parts, own_sums, held, down, pick)
    sums = reduce_stage(made, ["z", "x"], True)
    sums = reduce_stage([quarters(part) for part in sums], ["x", "z"], True)
    moe_out = reduce_stage([quarters(jnp.concatenate(sums, axis=1))], ["y"], False)[0]
    return attn_out, moe_out


def solution(mesh):
    fine = Mesh(mesh.devices.reshape(4, 4, 2, 4), ("z", "x", "core", "y"))
    dp = ("z", "x", "core")
    both = ("z", "x", "core", "y")
    return jax.shard_map(
        per_device,
        mesh=fine,
        in_specs=(
            P(both, None, None),
            P(both, None),
            P(),
            P(both, None),
            P(both, None),
            P(both, None),
            P(dp, None, "y"),
            P(dp, None, "y"),
            P(dp, "y", None),
        ),
        out_specs=(P(both, None, None), P(both, None)),
        check_vma=False,
    )
```

```python
import functools

import jax
import jax.numpy as jnp
from jax import lax
from jax.experimental import pallas as pl
from jax.experimental.pallas import tpu as pltpu
from jax.sharding import Mesh, PartitionSpec as P

WIDTH = 7168
LATENT = 512
KEY_DIM = 576
HEADS = 128
EXPERTS = 32
CTX = 4096
UNITS = 256
TOK = 8
CHIPS = 64
ROWS = CHIPS * TOK
PAY = WIDTH + 128
QK_SCALE = 192.0 ** (-0.5)
FAR_LOW = -1e30
ATT_ROWS = 1024
HALF = WIDTH // 2
K_STEP = 512
RETURN = (3328, 3840)
N_TILE = 1024
VMEM_LIMIT = 8 * 2**20
STEPS = HALF // K_STEP
D_STEP = WIDTH // STEPS
PART = ROWS // 4
GROUP = ROWS // 16
BF = jnp.bfloat16
F32 = jnp.float32


def attend_kernel(length_ref, query_ref, cache_ref, out_ref, top_ref, sum_ref, mix_ref):
    step = pl.program_id(0)
    length = length_ref[0]

    @pl.when(step == 0)
    def _():
        top_ref[...] = jnp.full_like(top_ref, FAR_LOW)
        sum_ref[...] = jnp.zeros_like(sum_ref)
        mix_ref[...] = jnp.zeros_like(mix_ref)

    @pl.when(step * ATT_ROWS < length)
    def _():
        rows = cache_ref[...]
        scores = QK_SCALE * lax.dot_general(
            query_ref[0], rows, (((0,), (0,)), ((), ())), preferred_element_type=F32
        )
        place = step * ATT_ROWS + lax.broadcasted_iota(jnp.int32, scores.shape, 1)
        scores = jnp.where(place < length, scores, FAR_LOW)
        top_old = top_ref[...]
        top_new = jnp.maximum(top_old, jnp.max(scores, axis=1, keepdims=True))
        weights = jnp.exp(scores - top_new)
        scale = jnp.exp(top_old - top_new)
        top_ref[...] = top_new
        sum_ref[...] = sum_ref[...] * scale + jnp.sum(weights, axis=1, keepdims=True)
        mix_ref[...] = mix_ref[...] * scale + lax.dot_general(
            weights.astype(BF), rows[:LATENT], (((1,), (1,)), ((), ())), preferred_element_type=F32
        )

    @pl.when(step == pl.num_programs(0) - 1)
    def _():
        out_ref[0] = (mix_ref[...] / sum_ref[...]).astype(BF)


def attend(length, query_rows, cache_latent):
    def cache_block(step, length_ref):
        return 0, jnp.minimum(step, (length_ref[0] - 1) // ATT_ROWS)

    return pl.pallas_call(
        attend_kernel,
        grid_spec=pltpu.PrefetchScalarGridSpec(
            num_scalar_prefetch=1,
            grid=(CTX // ATT_ROWS,),
            in_specs=[
                pl.BlockSpec((1, KEY_DIM, HEADS), lambda step, length_ref: (0, 0, 0)),
                pl.BlockSpec((KEY_DIM, ATT_ROWS), cache_block),
            ],
            out_specs=pl.BlockSpec((1, HEADS, LATENT), lambda step, length_ref: (0, 0, 0)),
            scratch_shapes=[
                pltpu.VMEM((HEADS, 1), F32),
                pltpu.VMEM((HEADS, 1), F32),
                pltpu.VMEM((HEADS, LATENT), F32),
            ],
        ),
        out_shape=jax.ShapeDtypeStruct((1, HEADS, LATENT), BF),
        compiler_params=pltpu.CompilerParams(vmem_limit_bytes=VMEM_LIMIT),
        cost_estimate=pl.CostEstimate(
            flops=2 * HEADS * CTX * (KEY_DIM + LATENT),
            bytes_accessed=4 * CTX * KEY_DIM * 2,
            transcendentals=HEADS * CTX,
        ),
        name="attend",
    )(length, jnp.swapaxes(query_rows, 1, 2), cache_latent.T)


def own_kernel(*refs):
    a_ref, b_ref, weights_a, weights_b = refs[0], refs[1], refs[2:6], refs[6:10]
    out_a, out_b, held = refs[10:]
    step = pl.program_id(0)

    @pl.when(step == 0)
    def _():
        out_a[...] = jnp.zeros_like(out_a)
        out_b[...] = jnp.zeros_like(out_b)

    for block, weights, out, start in ((a_ref, weights_a, out_a, 0), (b_ref, weights_b, out_b, HALF)):
        rows = pl.ds(pl.multiple_of(start + step * K_STEP, K_STEP), K_STEP)
        for place, weight in enumerate(weights):
            lanes = slice(place * UNITS, (place + 1) * UNITS)
            value = weight[...]
            held[rows, lanes] = value
            out[:, lanes] += jnp.dot(block[...], value, preferred_element_type=F32)


def keep_kernel(d_own, d_other, down):
    step = pl.program_id(0)
    columns = pl.ds(pl.multiple_of(step * D_STEP, D_STEP), D_STEP)
    down[:UNITS, columns] = d_own[...]
    down[UNITS:, columns] = d_other[...]


def keep(downs):
    return pl.pallas_call(
        keep_kernel,
        grid=(STEPS,),
        in_specs=[pl.BlockSpec((UNITS, D_STEP), lambda step: (0, step))] * 2,
        out_specs=pl.BlockSpec(memory_space=pltpu.VMEM),
        out_shape=pltpu.VMEM((2 * UNITS, WIDTH), BF),
        compiler_params=pltpu.CompilerParams(vmem_limit_bytes=VMEM_LIMIT),
        cost_estimate=pl.CostEstimate(
            flops=0, bytes_accessed=2 * 2 * UNITS * WIDTH, transcendentals=0
        ),
        name="keep",
    )(*downs)


def own_part(a_block, b_block, weights):
    block = pl.BlockSpec((PART, K_STEP), lambda step: (0, step))
    first = pl.BlockSpec((K_STEP, UNITS), lambda step: (step, 0))
    second = pl.BlockSpec((K_STEP, UNITS), lambda step: (step + STEPS, 0))
    sums = pl.BlockSpec((PART, 4 * UNITS), lambda step: (0, 0))
    return pl.pallas_call(
        own_kernel,
        grid=(STEPS,),
        in_specs=[block] * 2 + [first] * 4 + [second] * 4,
        out_specs=[sums] * 2 + [pl.BlockSpec(memory_space=pltpu.VMEM)],
        out_shape=[jax.ShapeDtypeStruct((PART, 4 * UNITS), F32)] * 2
        + [pltpu.VMEM((WIDTH, 4 * UNITS), BF)],
        compiler_params=pltpu.CompilerParams(vmem_limit_bytes=VMEM_LIMIT),
        cost_estimate=pl.CostEstimate(
            flops=2 * PART * WIDTH * 4 * UNITS,
            bytes_accessed=2 * (PART + 4 * UNITS) * WIDTH,
            transcendentals=0,
        ),
        name="own",
    )(a_block, b_block, *weights, *weights)


def on_chip(kernel, name, operands, shapes, flops, aliases=()):
    spec = pl.BlockSpec(memory_space=pltpu.VMEM)
    return pl.pallas_call(
        kernel,
        in_specs=[spec] * len(operands),
        out_specs=[spec] * len(shapes),
        out_shape=[pltpu.VMEM(*shape) for shape in shapes],
        compiler_params=pltpu.CompilerParams(vmem_limit_bytes=VMEM_LIMIT),
        cost_estimate=pl.CostEstimate(
            flops=flops, bytes_accessed=0, transcendentals=0
        ),
        input_output_aliases=dict(aliases),
        name=name,
    )(*operands)


def half_sums(blocks, held, start):
    stacked = jnp.concatenate([block[:, :HALF] for block in blocks], axis=0)
    return jnp.dot(stacked, held[start : start + HALF], preferred_element_type=F32)


def early_kernel(a1, b1, held, out_a, out_b, _):
    out_a[...] = half_sums([a1], held, 0)
    out_b[...] = half_sums([b1], held, HALF)


def late_kernel(a2, a3, b0, b1, b2, b3, held, pick, own_a, own_b, early_a, early_b, out_a, out_b):
    last_a = half_sums([a2, a3], held, 0)
    last_b = half_sums([b2, b3], held, HALF)

    def group(own, early, last, outer, inner):
        low = inner * GROUP
        if outer == 0:
            return own[low : low + GROUP]
        if outer == 1:
            return early[low : low + GROUP]
        low = low + (outer - 2) * PART
        return last[low : low + GROUP]

    for kx, tail in enumerate((b0, b1, b2, b3)):
        share = jnp.dot(tail[:, HALF:], pick[...], preferred_element_type=F32)
        for kz in range(4):
            total = group(own_a, early_a, last_a, kz, kx) + group(own_b, early_b, last_b, kx, kz)
            gate, up = total[:, : 2 * UNITS], total[:, 2 * UNITS :]
            made = gate / (1.0 + jnp.exp(-gate)) * up * share[kz * GROUP : (kz + 1) * GROUP]
            made = made.astype(BF)
            low_a, low_b = (kz * 4 + kx) * GROUP, (kx * 4 + kz) * GROUP
            out_a[low_a : low_a + GROUP, :] = made
            out_b[low_b : low_b + GROUP, :] = made


def down_kernel(low, high, hidden_a, hidden_b, down, *outs):
    count = high - low
    for half, hidden in enumerate((hidden_a, hidden_b)):
        for start in range(0, RETURN[half], N_TILE):
            stop = min(start + N_TILE, RETURN[half])
            column = half * RETURN[0]
            made = jnp.dot(
                hidden[low * PART : high * PART],
                down[:, column + start : column + stop],
                preferred_element_type=F32,
            ).astype(BF)
            for place in range(count):
                block = made[place * PART : (place + 1) * PART]
                outs[half * count + place][:, start:stop] = block


def early_part(a_block, b_block, held):
    sums = ((PART, 4 * UNITS), F32)
    return on_chip(
        early_kernel,
        "early",
        (a_block, b_block, held),
        (sums, sums, ((WIDTH, 4 * UNITS), BF)),
        2 * PART * WIDTH * 4 * UNITS,
        {2: 2},
    )


def sent_blocks(parts, own_sums, early_sums, held, down, pick):
    a_blocks, b_blocks = parts
    made = ((ROWS, 2 * UNITS), BF)
    halves = on_chip(
        late_kernel,
        "late",
        (*a_blocks[2:], *b_blocks, held, pick, *own_sums, *early_sums),
        (made, made),
        2 * 2 * PART * WIDTH * 4 * UNITS,
    )
    def some(low, high, hidden):
        count = high - low
        blocks = on_chip(
            functools.partial(down_kernel, low, high),
            "down",
            (*hidden, down),
            [((PART, width), BF) for width in RETURN for _ in range(count)],
            2 * count * PART * 2 * UNITS * WIDTH,
        )
        return blocks[:count], blocks[count:]

    (far_a, far_b), halves = lax.optimization_barrier((some(3, 4, halves), halves))
    rest_a, rest_b = some(0, 3, halves)
    return [[*rest_a, *far_a], [*rest_b, *far_b]]


def swap(array):
    return lax.ppermute(array, "core", [(0, 1), (1, 0)])


def move(array, axis, way):
    names = ("core", axis) if axis == "y" else (axis, "core")

    def flat(core, place):
        return core * 4 + place if axis == "y" else place * 2 + core

    pairs = [
        (flat(core, place), flat(core, (place + (way if core == 0 else -way)) % 4))
        for core in range(2)
        for place in range(4)
    ]
    return lax.ppermute(array, names, pairs)


def gather_stage(parts, axes):
    return [
        [part, move(part, axis, 1), move(part, axis, -1), move(part, axis, 2)]
        for part, axis in zip(parts, axes)
    ]


def joined(blocks):
    return jnp.concatenate(blocks, axis=0)


def added(*terms):
    total = terms[0].astype(F32)
    for term in terms[1:]:
        total = total + term.astype(F32)
    return total.astype(BF)


def reduce_stage(parts, axes, relay):
    if not relay:
        far = [move(blocks[3], axis, 2) for blocks, axis in zip(parts, axes)]
        near = [move(blocks[2], axis, 1) for blocks, axis in zip(parts, axes)]
        last = [move(blocks[1], axis, -1) for blocks, axis in zip(parts, axes)]
        return [
            added(blocks[0], n, l, f) for blocks, n, l, f in zip(parts, near, last, far)
        ]
    far = [move(blocks[3], axis, -1) for blocks, axis in zip(parts, axes)]
    near = [move(blocks[2], axis, 1) for blocks, axis in zip(parts, axes)]
    last = [
        move(added(blocks[1], relayed), axis, -1)
        for blocks, relayed, axis in zip(parts, far, axes)
    ]
    return [added(blocks[0], n, l) for blocks, n, l in zip(parts, near, last)]


def quarters(array):
    return jnp.split(array, 4, axis=0)


def payload_of(moe_input, expert_ids, gate_weights):
    chosen = expert_ids[:, :, None] == jnp.arange(EXPERTS, dtype=jnp.int32)
    shares = jnp.sum(jnp.where(chosen, gate_weights[:, :, None], 0.0), axis=1)
    high = lax.reduce_precision(shares, 8, 7)
    middle = lax.reduce_precision(shares - high, 8, 7)
    low = lax.reduce_precision(shares - high - middle, 8, 7)
    blank = jnp.zeros((TOK, 128 - 3 * EXPERTS), F32)
    tail = jnp.concatenate([high, middle, low, blank], axis=1).astype(BF)
    return jnp.concatenate([moe_input, tail], axis=1)


def per_device(
    query_rows,
    cache_latent,
    lengths,
    moe_input,
    expert_ids,
    gate_weights,
    expert_gate,
    expert_up,
    expert_down,
):
    chip = (lax.axis_index("z") * 4 + lax.axis_index("x")) * 2
    own = chip + lax.axis_index("core")
    other = chip + 1 - lax.axis_index("core")
    length = lax.dynamic_slice_in_dim(lengths, own * 4 + lax.axis_index("y"), 1)

    row = lax.broadcasted_iota(jnp.int32, (128, 2 * UNITS), 0)
    lane = lax.broadcasted_iota(jnp.int32, (128, 2 * UNITS), 1)
    wanted = jnp.where(lane < UNITS, own, other)
    pick = ((row % EXPERTS == wanted) & (row < 3 * EXPERTS)).astype(BF)

    payload = payload_of(moe_input, expert_ids, gate_weights)
    gate_own, up_own, down_own = expert_gate[0], expert_up[0], expert_down[0]
    column = joined(gather_stage([payload], ["y"])[0])
    column, gate_other, up_other = lax.optimization_barrier(
        (column, swap(gate_own), swap(up_own))
    )
    plane = gather_stage([column[:, :HALF], column[:, HALF:]], ["x", "z"])
    both = [joined(blocks) for blocks in plane]
    both, down_own, pick, length, query_rows = lax.optimization_barrier(
        (both, down_own, pick, length, query_rows)
    )
    down_other = swap(down_own)
    first = [move(part, axis, 1) for part, axis in zip(both, "zx")]
    attn_out = attend(length, query_rows, cache_latent)
    later, attn_out = lax.optimization_barrier((both, attn_out))
    second = [move(part, axis, -1) for part, axis in zip(later, "zx")]
    third = [move(part, axis, 1) for part, axis in zip(first, "zx")]
    parts = [list(blocks) for blocks in zip(both, first, second, third)]
    (a_own, b_own), (a_first, b_first), down_other = lax.optimization_barrier(
        (both, first, down_other)
    )
    *own_sums, held = own_part(a_own, b_own, (gate_own, gate_other, up_own, up_other))
    *early_sums, held = early_part(a_first, b_first, held)
    down = keep((down_own, down_other))
    early_sums, down = lax.optimization_barrier((early_sums, down))

    made = sent_blocks(parts, own_sums, early_sums, held, down, pick)
    sums = reduce_stage(made, ["z", "x"], True)
    sums = reduce_stage([quarters(part) for part in sums], ["x", "z"], True)
    moe_out = reduce_stage([quarters(jnp.concatenate(sums, axis=1))], ["y"], False)[0]
    return attn_out, moe_out


def solution(mesh):
    fine = Mesh(mesh.devices.reshape(4, 4, 2, 4), ("z", "x", "core", "y"))
    dp = ("z", "x", "core")
    both = ("z", "x", "core", "y")
    return jax.shard_map(
        per_device,
        mesh=fine,
        in_specs=(
            P(both, None, None),
            P(both, None),
            P(),
            P(both, None),
            P(both, None),
            P(both, None),
            P(dp, None, "y"),
            P(dp, None, "y"),
            P(dp, "y", None),
        ),
        out_specs=(P(both, None, None), P(both, None)),
        check_vma=False,
    )
```

```python
import functools

import jax
import jax.numpy as jnp
from jax import lax
from jax.experimental import pallas as pl
from jax.experimental.pallas import tpu as pltpu
from jax.sharding import Mesh, PartitionSpec as P

WIDTH = 7168
LATENT = 512
KEY_DIM = 576
HEADS = 128
EXPERTS = 32
CTX = 4096
UNITS = 256
TOK = 8
CHIPS = 64
ROWS = CHIPS * TOK
PAY = WIDTH + 128
QK_SCALE = 192.0 ** (-0.5)
FAR_LOW = -1e30
ATT_ROWS = 1024
HALF = WIDTH // 2
K_STEP = 512
RETURN = (3328, 3840)
N_TILE = 1024
VMEM_LIMIT = 8 * 2**20
STEPS = HALF // K_STEP
D_STEP = WIDTH // STEPS
PART = ROWS // 4
GROUP = ROWS // 16
BF = jnp.bfloat16
F32 = jnp.float32


def attend_kernel(length_ref, query_ref, cache_ref, out_ref, top_ref, sum_ref, mix_ref):
    step = pl.program_id(0)
    length = length_ref[0]

    @pl.when(step == 0)
    def _():
        top_ref[...] = jnp.full_like(top_ref, FAR_LOW)
        sum_ref[...] = jnp.zeros_like(sum_ref)
        mix_ref[...] = jnp.zeros_like(mix_ref)

    @pl.when(step * ATT_ROWS < length)
    def _():
        rows = cache_ref[...]
        scores = QK_SCALE * lax.dot_general(
            query_ref[0], rows, (((1,), (0,)), ((), ())), preferred_element_type=F32
        )
        place = step * ATT_ROWS + lax.broadcasted_iota(jnp.int32, scores.shape, 1)
        scores = jnp.where(place < length, scores, FAR_LOW)
        top_old = top_ref[...]
        top_new = jnp.maximum(top_old, jnp.max(scores, axis=1, keepdims=True))
        weights = jnp.exp(scores - top_new)
        scale = jnp.exp(top_old - top_new)
        top_ref[...] = top_new
        sum_ref[...] = sum_ref[...] * scale + jnp.sum(weights, axis=1, keepdims=True)
        mix_ref[...] = mix_ref[...] * scale + lax.dot_general(
            weights.astype(BF), rows[:LATENT], (((1,), (1,)), ((), ())), preferred_element_type=F32
        )

    @pl.when(step == pl.num_programs(0) - 1)
    def _():
        out_ref[0] = (mix_ref[...] / sum_ref[...]).astype(BF)


def attend(length, query_rows, cache_latent):
    def cache_block(step, length_ref):
        return 0, jnp.minimum(step, (length_ref[0] - 1) // ATT_ROWS)

    return pl.pallas_call(
        attend_kernel,
        grid_spec=pltpu.PrefetchScalarGridSpec(
            num_scalar_prefetch=1,
            grid=(CTX // ATT_ROWS,),
            in_specs=[
                pl.BlockSpec((1, HEADS, KEY_DIM), lambda step, length_ref: (0, 0, 0)),
                pl.BlockSpec((KEY_DIM, ATT_ROWS), cache_block),
            ],
            out_specs=pl.BlockSpec((1, HEADS, LATENT), lambda step, length_ref: (0, 0, 0)),
            scratch_shapes=[
                pltpu.VMEM((HEADS, 1), F32),
                pltpu.VMEM((HEADS, 1), F32),
                pltpu.VMEM((HEADS, LATENT), F32),
            ],
        ),
        out_shape=jax.ShapeDtypeStruct((1, HEADS, LATENT), BF),
        compiler_params=pltpu.CompilerParams(vmem_limit_bytes=VMEM_LIMIT),
        cost_estimate=pl.CostEstimate(
            flops=2 * HEADS * CTX * (KEY_DIM + LATENT),
            bytes_accessed=CTX * KEY_DIM * 2,
            transcendentals=HEADS * CTX,
        ),
        name="attend",
    )(length, query_rows, cache_latent.T)


def own_kernel(*refs):
    a_ref, b_ref, weights_a, weights_b, d_own, d_other = *refs[:2], refs[2:6], refs[6:10], *refs[10:12]
    out_a, out_b, held, down = refs[12:]
    step = pl.program_id(0)

    @pl.when(step == 0)
    def _():
        out_a[...] = jnp.zeros_like(out_a)
        out_b[...] = jnp.zeros_like(out_b)

    for block, weights, out, start in ((a_ref, weights_a, out_a, 0), (b_ref, weights_b, out_b, HALF)):
        rows = pl.ds(pl.multiple_of(start + step * K_STEP, K_STEP), K_STEP)
        for place, weight in enumerate(weights):
            lanes = slice(place * UNITS, (place + 1) * UNITS)
            value = weight[...]
            held[rows, lanes] = value
            out[:, lanes] += jnp.dot(block[...], value, preferred_element_type=F32)
    columns = pl.ds(pl.multiple_of(step * D_STEP, D_STEP), D_STEP)
    down[:UNITS, columns] = d_own[...]
    down[UNITS:, columns] = d_other[...]


def own_part(a_block, b_block, weights, downs):
    block = pl.BlockSpec((PART, K_STEP), lambda step: (0, step))
    first = pl.BlockSpec((K_STEP, UNITS), lambda step: (step, 0))
    second = pl.BlockSpec((K_STEP, UNITS), lambda step: (step + STEPS, 0))
    down = pl.BlockSpec((UNITS, D_STEP), lambda step: (0, step))
    sums = pl.BlockSpec((PART, 4 * UNITS), lambda step: (0, 0))
    return pl.pallas_call(
        own_kernel,
        grid=(STEPS,),
        in_specs=[block] * 2 + [first] * 4 + [second] * 4 + [down] * 2,
        out_specs=[sums] * 2 + [pl.BlockSpec(memory_space=pltpu.VMEM)] * 2,
        out_shape=[jax.ShapeDtypeStruct((PART, 4 * UNITS), F32)] * 2
        + [pltpu.VMEM((WIDTH, 4 * UNITS), BF), pltpu.VMEM((2 * UNITS, WIDTH), BF)],
        compiler_params=pltpu.CompilerParams(vmem_limit_bytes=VMEM_LIMIT),
        cost_estimate=pl.CostEstimate(
            flops=2 * PART * WIDTH * 4 * UNITS,
            bytes_accessed=2 * (PART + 6 * UNITS) * WIDTH,
            transcendentals=0,
        ),
        name="own",
    )(a_block, b_block, *weights, *weights, *downs)


def on_chip(kernel, name, operands, shapes, flops, aliases=()):
    spec = pl.BlockSpec(memory_space=pltpu.VMEM)
    return pl.pallas_call(
        kernel,
        in_specs=[spec] * len(operands),
        out_specs=[spec] * len(shapes),
        out_shape=[pltpu.VMEM(*shape) for shape in shapes],
        compiler_params=pltpu.CompilerParams(vmem_limit_bytes=VMEM_LIMIT),
        cost_estimate=pl.CostEstimate(flops=flops, bytes_accessed=0, transcendentals=0),
        input_output_aliases=dict(aliases),
        name=name,
    )(*operands)


def early_kernel(a1, a2, b1, b2, held, out_a, out_b, _):
    for blocks, out, start in (((a1, a2), out_a, 0), ((b1, b2), out_b, HALF)):
        stacked = jnp.concatenate([block[:, :HALF] for block in blocks], axis=0)
        out[...] = jnp.dot(stacked, held[start : start + HALF], preferred_element_type=F32)


def late_kernel(a3, b0, b1, b2, b3, held, pick, own_a, own_b, early_a, early_b, out_a, out_b):
    last_a = jnp.dot(a3[...], held[:HALF], preferred_element_type=F32)
    last_b = jnp.dot(b3[:, :HALF], held[HALF:], preferred_element_type=F32)

    def group(own, early, last, outer, inner):
        low = inner * GROUP
        if outer == 0:
            return own[low : low + GROUP]
        if outer == 3:
            return last[low : low + GROUP]
        low = low + (outer - 1) * PART
        return early[low : low + GROUP]

    for kx, tail in enumerate((b0, b1, b2, b3)):
        share = jnp.dot(tail[:, HALF:], pick[...], preferred_element_type=F32)
        for kz in range(4):
            total = group(own_a, early_a, last_a, kz, kx) + group(own_b, early_b, last_b, kx, kz)
            gate, up = total[:, : 2 * UNITS], total[:, 2 * UNITS :]
            made = gate / (1.0 + jnp.exp(-gate)) * up * share[kz * GROUP : (kz + 1) * GROUP]
            made = made.astype(BF)
            low_a, low_b = (kz * 4 + kx) * GROUP, (kx * 4 + kz) * GROUP
            out_a[low_a : low_a + GROUP, :] = made
            out_b[low_b : low_b + GROUP, :] = made


def down_kernel(low, high, hidden_a, hidden_b, down, *outs):
    count = high - low
    for half, hidden in enumerate((hidden_a, hidden_b)):
        for start in range(0, RETURN[half], N_TILE):
            stop = min(start + N_TILE, RETURN[half])
            column = half * RETURN[0]
            made = jnp.dot(
                hidden[low * PART : high * PART],
                down[:, column + start : column + stop],
                preferred_element_type=F32,
            ).astype(BF)
            for place in range(count):
                block = made[place * PART : (place + 1) * PART]
                outs[half * count + place][:, start:stop] = block


def sent_blocks(parts, own_sums, held, down, pick):
    a_blocks, b_blocks = parts
    sums = ((2 * PART, 4 * UNITS), F32)
    *early_sums, held = on_chip(
        early_kernel,
        "early",
        (*a_blocks[1:3], *b_blocks[1:3], held),
        (sums, sums, ((WIDTH, 4 * UNITS), BF)),
        2 * 2 * PART * WIDTH * 4 * UNITS,
        {4: 2},
    )
    made = ((ROWS, 2 * UNITS), BF)
    halves = on_chip(
        late_kernel,
        "late",
        (a_blocks[3], *b_blocks, held, pick, *own_sums, *early_sums),
        (made, made),
        2 * PART * WIDTH * 4 * UNITS,
    )
    def some(low, high, hidden):
        count = high - low
        blocks = on_chip(
            functools.partial(down_kernel, low, high),
            "down",
            (*hidden, down),
            [((PART, width), BF) for width in RETURN for _ in range(count)],
            2 * count * PART * 2 * UNITS * WIDTH,
        )
        return blocks[:count], blocks[count:]

    (far_a, far_b), halves = lax.optimization_barrier((some(3, 4, halves), halves))
    rest_a, rest_b = some(0, 3, halves)
    return [[*rest_a, *far_a], [*rest_b, *far_b]]


def swap(array):
    return lax.ppermute(array, "core", [(0, 1), (1, 0)])


def move(array, axis, way):
    names = ("core", axis) if axis == "y" else (axis, "core")

    def flat(core, place):
        return core * 4 + place if axis == "y" else place * 2 + core

    pairs = [
        (flat(core, place), flat(core, (place + (way if core == 0 else -way)) % 4))
        for core in range(2)
        for place in range(4)
    ]
    return lax.ppermute(array, names, pairs)


def gather_stage(parts, axes):
    return [
        [part, move(part, axis, 1), move(part, axis, -1), move(part, axis, 2)]
        for part, axis in zip(parts, axes)
    ]


def joined(blocks):
    return jnp.concatenate(blocks, axis=0)


def added(*terms):
    total = terms[0].astype(F32)
    for term in terms[1:]:
        total = total + term.astype(F32)
    return total.astype(BF)


def reduce_stage(parts, axes, relay):
    if not relay:
        far = [move(blocks[3], axis, 2) for blocks, axis in zip(parts, axes)]
        near = [move(blocks[2], axis, 1) for blocks, axis in zip(parts, axes)]
        last = [move(blocks[1], axis, -1) for blocks, axis in zip(parts, axes)]
        return [
            added(blocks[0], n, l, f) for blocks, n, l, f in zip(parts, near, last, far)
        ]
    far = [move(blocks[3], axis, -1) for blocks, axis in zip(parts, axes)]
    near = [move(blocks[2], axis, 1) for blocks, axis in zip(parts, axes)]
    last = [
        move(added(blocks[1], relayed), axis, -1)
        for blocks, relayed, axis in zip(parts, far, axes)
    ]
    return [added(blocks[0], n, l) for blocks, n, l in zip(parts, near, last)]


def quarters(array):
    return jnp.split(array, 4, axis=0)


def payload_of(moe_input, expert_ids, gate_weights):
    chosen = expert_ids[:, :, None] == jnp.arange(EXPERTS, dtype=jnp.int32)
    shares = jnp.sum(jnp.where(chosen, gate_weights[:, :, None], 0.0), axis=1)
    high = lax.reduce_precision(shares, 8, 7)
    middle = lax.reduce_precision(shares - high, 8, 7)
    low = lax.reduce_precision(shares - high - middle, 8, 7)
    blank = jnp.zeros((TOK, 128 - 3 * EXPERTS), F32)
    tail = jnp.concatenate([high, middle, low, blank], axis=1).astype(BF)
    return jnp.concatenate([moe_input, tail], axis=1)


def per_device(
    query_rows,
    cache_latent,
    lengths,
    moe_input,
    expert_ids,
    gate_weights,
    expert_gate,
    expert_up,
    expert_down,
):
    chip = (lax.axis_index("z") * 4 + lax.axis_index("x")) * 2
    own = chip + lax.axis_index("core")
    other = chip + 1 - lax.axis_index("core")
    length = lax.dynamic_slice_in_dim(lengths, own * 4 + lax.axis_index("y"), 1)

    row = lax.broadcasted_iota(jnp.int32, (128, 2 * UNITS), 0)
    lane = lax.broadcasted_iota(jnp.int32, (128, 2 * UNITS), 1)
    wanted = jnp.where(lane < UNITS, own, other)
    pick = ((row % EXPERTS == wanted) & (row < 3 * EXPERTS)).astype(BF)

    payload = payload_of(moe_input, expert_ids, gate_weights)
    gate_own, up_own, down_own = expert_gate[0], expert_up[0], expert_down[0]
    column = joined(gather_stage([payload], ["y"])[0])
    column, gate_other, up_other = lax.optimization_barrier(
        (column, swap(gate_own), swap(up_own))
    )
    plane = gather_stage([column[:, :HALF], column[:, HALF:]], ["x", "z"])
    both = [joined(blocks) for blocks in plane]
    both, query_rows, down_own, pick, length = lax.optimization_barrier(
        (both, query_rows, down_own, pick, length)
    )
    down_other = swap(down_own)
    first = [move(part, axis, 1) for part, axis in zip(both, "zx")]
    second = [move(part, axis, -1) for part, axis in zip(both, "zx")]
    attn_out = attend(length, query_rows, cache_latent)
    *own_sums, held, down = own_part(
        both[0], both[1], (gate_own, gate_other, up_own, up_other), (down_own, down_other)
    )
    first, attn_out, own_sums = lax.optimization_barrier((first, attn_out, own_sums))
    third = [move(part, axis, 1) for part, axis in zip(first, "zx")]
    parts = [list(blocks) for blocks in zip(both, first, second, third)]

    made = sent_blocks(parts, own_sums, held, down, pick)
    sums = reduce_stage(made, ["z", "x"], True)
    sums = reduce_stage([quarters(part) for part in sums], ["x", "z"], True)
    moe_out = reduce_stage([quarters(jnp.concatenate(sums, axis=1))], ["y"], False)[0]
    return attn_out, moe_out


def solution(mesh):
    fine = Mesh(mesh.devices.reshape(4, 4, 2, 4), ("z", "x", "core", "y"))
    dp = ("z", "x", "core")
    both = ("z", "x", "core", "y")
    return jax.shard_map(
        per_device,
        mesh=fine,
        in_specs=(
            P(both, None, None),
            P(both, None),
            P(),
            P(both, None),
            P(both, None),
            P(both, None),
            P(dp, None, "y"),
            P(dp, None, "y"),
            P(dp, "y", None),
        ),
        out_specs=(P(both, None, None), P(both, None)),
        check_vma=False,
    )
```
